32 devices in a mesh: pole: 2 (over x), row: 8 (over z, y), col: 2 (over core).
Axes of the slice: x: 2, y: 2, z: 4, core: 2. Of those that a mesh axis runs over, the one named last changes fastest.
Arguments:
- ancestor_inverse: float32 [2, 24576, 12288], P(None, ('pole', 'row'), 'col'), parts along dimension 1, may hold values from -6 to 6
- factor_panels: float32 [4, 2, 24576, 128], P(None, None, ('pole', 'col', 'row')), parts along dimension 2, may hold values from -0.0546875 to 0.0546875
- diag_inverse: float32 [8, 2, 128, 128], P('pole'), parts along dimension 0, may hold values from -6 to 6
- coupling: float32 [4, 2, 128, 128], P('pole'), parts along dimension 0, may hold values from -0.5 to 0.5
- block_pattern: int32 [4, 96], replicated, may hold values from 0 to 1, as said below
- tree_order: int32 [4], replicated, may hold values from 0 to 3, each once
Outputs:
- inverse_panels: float32 [4, 2, 24576, 128], P(None, None, ('pole', 'row')), parts along dimension 2
- inverse_diagonal: float32 [8, 2, 128, 128], P('pole'), parts along dimension 0
- inverse_coupling: float32 [4, 2, 128, 128], P('pole'), parts along dimension 0
The draws below stay inside these ranges and needn't reach their ends.
There are 2 independent parts, one for each index of `pole`. The reference program is written for one: setup_inputs(seed, part) draws one part's arguments, and reference() takes and returns one part's arrays. A program takes and returns all parts, laid end to end along the dimension named above; an argument that names none is the same for every part. Nothing has to cross between parts.
Inputs may be any that keep to these rules, and one draw needn't show every extreme that they name: `tree_order`: each supernode number appears once. `block_pattern`: blocks 0 and 48 lie in every supernode's structure.
All inputs are finite; a program needn't handle non-finite values.
Results may differ from the reference program's by a relative error of at most 0.0001.
Values sent between devices are 32-bit elements; how exact they have to be, the bound alone decides.
No kernel may reach another device: no remote copies, remote signals or barrier semaphores. Data moves between devices by JAX's collectives and lax.ppermute only.
A program may use at most 192 MiB of HBM per device.

```python
import jax
import jax.numpy as jnp
from jax import lax

B = 128
ANC = 12288
SUPER = 4
NB = 96


def draw_block_pattern(key, part):
    random_level = jax.random.randint(key, (SUPER, NB), 0, 8)
    pattern_live = (random_level < 5).astype(jnp.int32)
    block_index = jnp.arange(NB, dtype=jnp.int32)
    forced_blocks = ((block_index == 0) | (block_index == NB // 2)).astype(jnp.int32)
    return jnp.maximum(pattern_live, forced_blocks[None, :])


def block_levels(rng, extent, cuts, least, high):
    loudness, own = 1.0, jax.random.fold_in(rng, 6)
    for axis_at, shards_of in cuts:
        draws = jnp.exp(jax.random.uniform(jax.random.fold_in(own, axis_at), (shards_of,), jnp.float32, least / len(cuts), high / len(cuts)))
        loudness = loudness * jnp.repeat(draws, extent[axis_at] // shards_of).reshape([-1 if axis == axis_at else 1 for axis in range(len(extent))])
    return loudness


def normal_values(key, shape, width, reach, shards=(), kind=jnp.bfloat16):
    gain = block_levels(key, shape, shards, -0.22, 0.18) if shards else 1.0
    array = jax.random.normal(key, shape, jnp.float32) * width * gain
    return jnp.minimum(jnp.maximum(array, -reach), reach).astype(kind)


def setup_inputs(seed: int = 0, part: int = 0) -> dict:
    splits = jax.random.split(jax.random.key(seed), 7)
    part_splits = jax.random.split(jax.random.fold_in(splits[6], part), 7)
    ancestor_inverse = normal_values(part_splits[0], (2, ANC, ANC), 1.0, 6.0, ((1, 8), (2, 2)), jnp.float32)
    factor_panels = normal_values(part_splits[1], (SUPER, 2, ANC, B), ANC ** -0.5, 0.0546875, ((2, 16),), jnp.float32)
    diag_inverse = normal_values(part_splits[2], (SUPER, 2, B, B), 1.0, 6.0, (), jnp.float32)
    coupling = normal_values(part_splits[3], (SUPER // 2, 2, B, B), B ** -0.5, 0.5, (), jnp.float32)
    block_pattern = draw_block_pattern(jax.random.fold_in(splits[6], 71), part)
    tree_order = jax.random.permutation(splits[5], SUPER).astype(jnp.int32)
    return {"ancestor_inverse": ancestor_inverse, "factor_panels": factor_panels, "diag_inverse": diag_inverse, "coupling": coupling, "block_pattern": block_pattern, "tree_order": tree_order}


def matmul(left_side, right_side):
    return jnp.dot(left_side, right_side, preferred_element_type=jnp.float32, precision=lax.Precision.HIGHEST)


def multiply(left_side, right_side):
    real_part = matmul(left_side[0], right_side[0]) - matmul(left_side[1], right_side[1])
    imag_part = matmul(left_side[0], right_side[1]) + matmul(left_side[1], right_side[0])
    return jnp.stack([real_part, imag_part])


def flipped(matrix):
    return jnp.swapaxes(matrix, 1, 2)


def reference(ancestor_inverse, factor_panels, diag_inverse, coupling, block_pattern, tree_order):
    row_masks = jnp.repeat(block_pattern.astype(jnp.float32), B, axis=1)
    sorted_masks = jnp.take(row_masks, tree_order, axis=0)
    masks = jnp.concatenate([sorted_masks[:2], sorted_masks[2:] * sorted_masks[:2]], axis=0)
    panels = jnp.take(factor_panels, tree_order, axis=0) * masks[:, None, :, None]
    diag_blocks = jnp.take(diag_inverse, tree_order, axis=0)
    parent_cols = []
    parent_diag = []
    for tree_slot in range(2):
        column_block = -masks[tree_slot][None, :, None] * multiply(ancestor_inverse, panels[tree_slot])
        parent_cols.append(column_block)
        parent_diag.append(diag_blocks[tree_slot] - multiply(flipped(panels[tree_slot]), column_block))
    child_cols = []
    child_diag = []
    crosses = []
    for tree_slot in range(2):
        child_slot = tree_slot + 2
        link_block = coupling[tree_slot]
        column_block = -masks[child_slot][None, :, None] * (
            multiply(ancestor_inverse, panels[child_slot]) + multiply(parent_cols[tree_slot], link_block))
        cross_block = -(multiply(flipped(parent_cols[tree_slot]), panels[child_slot])
                        + multiply(parent_diag[tree_slot], link_block))
        child_cols.append(column_block)
        crosses.append(cross_block)
        child_diag.append(diag_blocks[child_slot] - multiply(flipped(panels[child_slot]), column_block)
                          - multiply(flipped(link_block), cross_block))
    all_cols = jnp.stack(parent_cols + child_cols)
    all_diag = jnp.stack(parent_diag + child_diag)
    inverse_panels = jnp.zeros_like(factor_panels).at[tree_order].set(all_cols)
    inverse_diagonal = jnp.zeros_like(diag_inverse).at[tree_order].set(all_diag)
    return inverse_panels, inverse_diagonal, jnp.stack(crosses)
```

```python
import functools

import jax
import jax.numpy as jnp
from jax import lax
from jax.experimental import pallas as pl
from jax.experimental.pallas import tpu as pltpu
from jax.sharding import PartitionSpec as P


def matmul(left_side, right_side):
    return jnp.dot(
        left_side, right_side, preferred_element_type=jnp.float32, precision=lax.Precision.HIGHEST
    )


def multiply(left_side, right_side):
    real_part = matmul(left_side[0], right_side[0]) - matmul(left_side[1], right_side[1])
    imag_part = matmul(left_side[0], right_side[1]) + matmul(left_side[1], right_side[0])
    return jnp.stack([real_part, imag_part])


def flipped(matrix):
    return jnp.swapaxes(matrix, 1, 2)


def halves(value):
    high = value.astype(jnp.bfloat16)
    low = (value - high.astype(jnp.float32)).astype(jnp.bfloat16)
    return high, low


def dot32(left_side, right_side, contract=((1,), (0,))):
    return lax.dot_general(
        left_side, right_side, (contract, ((), ())), preferred_element_type=jnp.float32
    )


def dot3(left_side, right_side, contract=((1,), (0,))):
    return (
        dot32(left_side[0], right_side[0], contract)
        + dot32(left_side[0], right_side[1], contract)
        + dot32(left_side[1], right_side[0], contract)
    )


ARRIVALS = (
    ("own", False, (0, 1, 2, 3)),
    ("right 1", False, (None, 0, 1, 2)),
    ("left 1", False, (1, 2, 3, None)),
    ("over 1", True, (0, 1, 2, 3)),
    ("right 2", (False, True, False, False), (None, 0, 0, 1)),
    ("left 2", (False, False, True, False), (2, 3, 3, None)),
    ("over 2", True, (1, 2, 1, 2)),
    ("right 3", False, (None, None, None, 0)),
    ("left 3", False, (3, None, None, None)),
    ("over 3", True, (2, 3, 0, 1)),
    ("over 4", True, (3, None, None, 0)),
)
LINES = len(ARRIVALS[0][2])


class Layout:
    def __init__(self, rows, cols, a_shape, p_shape):
        self.rows, self.cols = rows, cols
        self.lines = rows // 2
        self.slots, _, self.piece_rows, self.block = p_shape
        self.tile_rows, self.half_rows = a_shape[1:]
        self.piece_blocks = self.piece_rows // self.block
        self.tile_blocks = self.tile_rows // self.block
        self.half_blocks = self.half_rows // self.block
        self.units = self.piece_blocks * self.slots
        self.buffers = len(ARRIVALS)
        self.group = next(size for size in (4, 3, 2, 1) if self.tile_blocks % size == 0)
        self.ranks = 0
        self.source = cols * rows * self.units
        self.order = self.source + self.units
        self.live = self.order + self.slots * self.tile_blocks
        self.owners = self.live + self.slots
        self.windows = self.owners + self.buffers
        self.most = self.windows + 2
        self.total = self.most + 1


def plan_kernel(layout, place, pattern, order, plan):
    row, col = place[0], place[1]
    trees = layout.slots // 2
    names = [order[slot] for slot in range(layout.slots)]

    def live(slot, block):
        value = pattern[names[slot], block]
        if slot >= trees:
            value = value * pattern[names[slot - trees], block]
        return value

    def of_owner(owner, most):
        count = jnp.int32(0)
        for piece in range(layout.piece_blocks):
            for slot in range(layout.slots):
                value = live(slot, owner * layout.piece_blocks + piece)
                at = owner * layout.units + piece * layout.slots + slot
                plan[layout.ranks + at] = jnp.where(value > 0, count, -1)
                count = count + value
        return jnp.maximum(most, count)

    plan[layout.most] = lax.fori_loop(0, layout.cols * layout.rows, of_owner, jnp.int32(0))
    for unit in range(layout.units):
        plan[layout.source + unit] = 0
    mine = (col * layout.rows + row) * layout.units
    for unit in range(layout.units):
        rank = plan[layout.ranks + mine + unit]

        @pl.when(rank >= 0)
        def _():
            plan[layout.source + rank] = unit

    for slot in range(layout.slots):
        count = jnp.int32(0)
        values = []
        for index in range(layout.tile_blocks):
            value = live(slot, row * layout.tile_blocks + index)
            values.append(value)
            count = count + value
        plan[layout.live + slot] = count
        front, back = jnp.int32(0), count
        for index, value in enumerate(values):
            at = layout.order + slot * layout.tile_blocks + jnp.where(value > 0, front, back)
            plan[at] = index
            front, back = front + value, back + 1 - value

    line, side = row // 2, row % 2
    window_line = (row * layout.tile_blocks % layout.half_blocks) // layout.piece_blocks // 2
    windows = [jnp.int32(0), jnp.int32(0)]
    for index, (_, across, origins) in enumerate(ARRIVALS):
        owner = jnp.int32(-1)
        for at, origin in enumerate(origins):
            if origin is not None:
                crossed = across if isinstance(across, bool) else across[at]
                from_side = 1 - side if crossed else side
                owner = jnp.where(line == at, origin * 2 + from_side, owner)
        plan[layout.owners + index] = owner
        for which in range(2):
            hit = owner == window_line * 2 + which
            windows[which] = jnp.where(hit, index, windows[which])
    for which in range(2):
        plan[layout.windows + which] = windows[which]


def make_plan(layout, row, col, block_pattern, tree_order):
    smem = pl.BlockSpec(memory_space=pltpu.SMEM)
    return pl.pallas_call(
        functools.partial(plan_kernel, layout),
        out_shape=jax.ShapeDtypeStruct((layout.total,), jnp.int32),
        in_specs=[smem] * 3,
        out_specs=smem,
        name="make_plan",
    )(jnp.stack([row, col]).astype(jnp.int32), block_pattern, tree_order)


def compact_kernel(layout, plan, order, panels, units, sems):
    block = layout.block
    copies = []
    for unit in range(units.shape[0]):
        source = plan[layout.source + unit]
        first = pl.multiple_of(source // layout.slots * block, block)
        copy = pltpu.make_async_copy(
            panels.at[order[source % layout.slots], :, pl.ds(first, block), :],
            units.at[unit],
            sems.at[unit],
        )
        copy.start()
        copies.append(copy)
    for copy in copies:
        copy.wait()


def compact_units(layout, plan, tree_order, panels):
    shape = (layout.units, 2, layout.block, layout.block)
    return pl.pallas_call(
        functools.partial(compact_kernel, layout),
        out_shape=jax.ShapeDtypeStruct(shape, jnp.float32),
        grid_spec=pltpu.PrefetchScalarGridSpec(
            num_scalar_prefetch=2,
            grid=(1,),
            in_specs=[pl.BlockSpec(memory_space=pltpu.HBM)],
            out_specs=pl.BlockSpec(shape, lambda step, plan, order: (0, 0, 0, 0)),
            scratch_shapes=[pltpu.SemaphoreType.DMA((layout.units,))],
        ),
        compiler_params=pltpu.CompilerParams(vmem_limit_bytes=16 * 2**20),
        name="compact_units",
    )(plan, tree_order, panels)


def owner_at(layout, which, plan, step):
    owner = plan[layout.owners + which[0]]
    for local in range(1, len(which)):
        later = step // layout.piece_blocks >= local
        owner = jnp.where(later, plan[layout.owners + which[local]], owner)
    return owner


def gemm_kernel(layout, which, first_call, plan, place, *refs):
    refs = list(refs)
    in_ref = None if first_call else refs.pop(0)
    a_ref = refs.pop(0)
    units = refs[: len(which)]
    out_ref, total, a_parts, weights, sem = refs[len(which) :]
    step = pl.program_id(0)
    block, group = layout.block, layout.group
    width = 2 * block
    rows = layout.tile_rows
    span_rows = group * block

    @pl.when(step == 0)
    def _():
        if first_call:
            total[...] = jnp.zeros_like(total)
        else:
            load = pltpu.make_async_copy(in_ref, total, sem)
            load.start()
            load.wait()

    owner = owner_at(layout, which, plan, step)

    @pl.loop(0, jnp.where(owner >= 0, rows // block, 0))
    def _(index):
        span = pl.ds(pl.multiple_of(index * block, block), block)
        for part in range(2):
            high, low = halves(a_ref[part, span, :])
            a_parts[span, part * block : (part + 1) * block] = high
            a_parts[span, width + part * block : width + (part + 1) * block] = low
            a_parts[span, 2 * width + part * block : 2 * width + (part + 1) * block] = high

    base = place[1] * layout.rows * layout.units + owner * layout.units
    base = base + step % layout.piece_blocks * layout.slots

    @pl.loop(0, jnp.where(owner >= 0, layout.slots, 0))
    def _(slot):
        rank = plan[layout.ranks + base + slot]

        for local in range(len(which)):

            @pl.when((rank >= 0) & (step // layout.piece_blocks == local))
            def _():
                real, imag = units[local][rank, 0], units[local][rank, 1]
                real_parts, imag_parts = halves(real), halves(imag)
                for third, part in enumerate((0, 0, 1)):
                    top = third * width
                    weights[top : top + block, :block] = real_parts[part]
                    weights[top : top + block, block:] = imag_parts[part]
                    weights[top + block : top + width, :block] = -imag_parts[part]
                    weights[top + block : top + width, block:] = real_parts[part]

        count = plan[layout.live + slot]

        @pl.loop(0, jnp.where(rank >= 0, (count + group - 1) // group, 0))
        def _(index):
            spans = []
            for at in range(group):
                first = plan[layout.order + slot * layout.tile_blocks + index * group + at]
                spans.append(pl.ds(pl.multiple_of(first * block, block), block))
            left_side = jnp.concatenate([a_parts[span, :] for span in spans], axis=0)
            product = dot32(left_side, weights[...])
            for at, span in enumerate(spans):
                total[slot, span, :] += product[at * block : (at + 1) * block]

    @pl.when(step == pl.num_programs(0) - 1)
    def _():
        store = pltpu.make_async_copy(total, out_ref, sem)
        store.start()
        store.wait()


def gemm_units(layout, plan, place, total, ancestor_inverse, buffers, which):
    first_call = total is None
    totals = [] if first_call else [total]
    hbm = pl.BlockSpec(memory_space=pltpu.HBM)
    block, pieces = layout.block, layout.piece_blocks
    rows, width = layout.tile_rows, 2 * layout.block

    def column(step, plan, place):
        owner = owner_at(layout, which, plan, step)
        return 0, 0, jnp.where(owner >= 0, owner * pieces + step % pieces, 0)

    shape = (layout.slots, rows, width)
    steps = len(which) * pieces
    return pl.pallas_call(
        functools.partial(gemm_kernel, layout, which, first_call),
        out_shape=jax.ShapeDtypeStruct(shape, jnp.float32),
        grid_spec=pltpu.PrefetchScalarGridSpec(
            num_scalar_prefetch=2,
            grid=(steps,),
            in_specs=[hbm] * len(totals)
            + [pl.BlockSpec((2, rows, block), column)]
            + [
                pl.BlockSpec(
                    buffer.shape,
                    lambda step, plan, place: (0, 0, 0, 0),
                    pipeline_mode=pl.Buffered(1),
                )
                for buffer in buffers
            ],
            out_specs=hbm,
            scratch_shapes=[
                pltpu.VMEM(shape, jnp.float32),
                pltpu.VMEM((rows, 3 * width), jnp.bfloat16),
                pltpu.VMEM((3 * width, width), jnp.bfloat16),
                pltpu.SemaphoreType.DMA,
            ],
        ),
        input_output_aliases={} if first_call else {2: 0},
        compiler_params=pltpu.CompilerParams(vmem_limit_bytes=30 * 2**20),
        cost_estimate=pl.CostEstimate(
            flops=steps * layout.slots * 3 * 2 * rows * width * width // 2,
            bytes_accessed=steps * rows * block * 8 + 8 * layout.slots * rows * width,
            transcendentals=0,
        ),
        name="gemm_units",
    )(plan, place, *totals, ancestor_inverse, *buffers)


def finish_kernel(layout, step_blocks, plan, place, order, mine, other, coupling, *refs):
    buffers = refs[: layout.buffers]
    columns, sums, acc, held, sems = refs[layout.buffers :]
    step = pl.program_id(0)
    block, slots, trees = layout.block, layout.slots, layout.slots // 2
    row, col = place[0], place[1]
    holds = row * layout.tile_blocks // layout.half_blocks == col
    inner = row * layout.tile_blocks % layout.half_blocks
    base = col * layout.rows * layout.units + inner * slots

    def fetch(which, index):
        return pltpu.make_async_copy(buffers[index], held.at[which], sems.at[which])

    @pl.when(step == 0)
    def _():
        acc[...] = jnp.zeros_like(acc)
        for act in ("start", "wait"):
            for which in range(2):
                for index in range(layout.buffers):

                    @pl.when(holds & (plan[layout.windows + which] == index))
                    def _():
                        getattr(fetch(which, index), act)()

    def window(slot):
        parts = []
        for at in range(step_blocks):
            index = step * step_blocks + at
            rank = plan[layout.ranks + base + index * slots + slot]
            which, place_in = index // layout.piece_blocks, jnp.maximum(rank, 0)
            unit = held[which, place_in]
            whole = jnp.concatenate([unit[0], unit[1]], axis=1)
            parts.append(jnp.where(rank >= 0, whole, 0.0))
        return halves(jnp.concatenate(parts, axis=0))

    def masked(slot, value):
        parts = []
        for at in range(step_blocks):
            alive = is_live(slot, step * step_blocks + at)
            parts.append(jnp.where(alive, -value[at * block : (at + 1) * block], 0.0))
        return jnp.concatenate(parts, axis=0)

    def is_live(slot, index):
        alive = jnp.bool_(False)
        for at in range(layout.tile_blocks):
            found = plan[layout.order + slot * layout.tile_blocks + at] == index
            alive = alive | (found & (at < plan[layout.live + slot]))
        return alive

    def put(slot, value):
        columns[order[slot], 0] = value[:, :block]
        columns[order[slot], 1] = value[:, block:]

    rows_first = ((0,), (0,))
    for tree in range(trees):
        child = tree + trees
        real, imag = coupling[tree, 0], coupling[tree, 1]
        link = jnp.concatenate(
            [jnp.concatenate([real, imag], axis=1), jnp.concatenate([-imag, real], axis=1)], axis=0
        )
        parent_col = masked(tree, mine[tree] + other[tree])
        put(tree, parent_col)
        parent_parts = halves(parent_col)
        linked = dot3(parent_parts, halves(link))
        child_col = masked(child, mine[child] + other[child] + linked)
        put(child, child_col)

        @pl.when(holds)
        def _():
            child_panel = window(child)
            acc[3 * tree] += dot3(window(tree), parent_parts, rows_first)
            acc[3 * tree + 1] += dot3(child_panel, parent_parts, rows_first)
            acc[3 * tree + 2] += dot3(child_panel, halves(child_col), rows_first)

    @pl.when(step == pl.num_programs(0) - 1)
    def _():
        for index in range(3 * trees):
            value = acc[index]
            sums[index, 0] = value[:block, :block] - value[block:, block:]
            sums[index, 1] = value[:block, block:] + value[block:, :block]


def finish_columns(layout, plan, place, tree_order, mine, other, coupling, buffers):
    block, slots = layout.block, layout.slots
    rows, width = layout.tile_rows, 2 * layout.block
    step_blocks = 2 if layout.piece_blocks % 2 == 0 else 1
    step_rows = step_blocks * block
    half = pl.BlockSpec((slots, step_rows, width), lambda step, *_: (0, step, 0))
    sums_shape = (3 * slots // 2, 2, block, block)
    return pl.pallas_call(
        functools.partial(finish_kernel, layout, step_blocks),
        out_shape=(
            jax.ShapeDtypeStruct((slots, 2, rows, block), jnp.float32),
            jax.ShapeDtypeStruct(sums_shape, jnp.float32),
        ),
        grid_spec=pltpu.PrefetchScalarGridSpec(
            num_scalar_prefetch=3,
            grid=(rows // step_rows,),
            in_specs=[half, half, pl.BlockSpec(coupling.shape, lambda step, *_: (0, 0, 0, 0))]
            + [pl.BlockSpec(memory_space=pl.ANY)] * layout.buffers,
            out_specs=[
                pl.BlockSpec((slots, 2, step_rows, block), lambda step, *_: (0, 0, step, 0)),
                pl.BlockSpec(sums_shape, lambda step, *_: (0, 0, 0, 0)),
            ],
            scratch_shapes=[
                pltpu.VMEM((3 * slots // 2, width, width), jnp.float32),
                pltpu.VMEM((2,) + buffers[0].shape, jnp.float32),
                pltpu.SemaphoreType.DMA((2,)),
            ],
        ),
        compiler_params=pltpu.CompilerParams(vmem_limit_bytes=24 * 2**20),
        name="finish_columns",
    )(plan, place, tree_order, mine, other, coupling, *buffers)


def complex_dot(left_side, right_side, contract=((1,), (0,))):
    def dot(left_part, right_part):
        return dot3(halves(left_side[left_part]), halves(right_side[right_part]), contract)

    return dot(0, 0) - dot(1, 1), dot(0, 1) + dot(1, 0)


def diagonal_kernel(order, sums, diag_in, coupling, diag_out, cross_out):
    trees = coupling.shape[0]
    for tree in range(trees):
        parent, child = order[tree], order[tree + trees]
        link = (coupling[tree, 0], coupling[tree, 1])
        parent_diag = tuple(diag_in[parent, part] - sums[3 * tree, part] for part in range(2))
        moved = complex_dot(parent_diag, link)
        cross = tuple(-(sums[3 * tree + 1, part].T + moved[part]) for part in range(2))
        back = complex_dot(link, cross, ((0,), (0,)))
        for part in range(2):
            diag_out[parent, part] = parent_diag[part]
            cross_out[tree, part] = cross[part]
            diag_out[child, part] = diag_in[child, part] - sums[3 * tree + 2, part] - back[part]


def finish_diagonals(order, sums, diag_inverse, coupling):
    vmem = pl.BlockSpec(memory_space=pltpu.VMEM)
    return pl.pallas_call(
        diagonal_kernel,
        out_shape=(
            jax.ShapeDtypeStruct(diag_inverse.shape, jnp.float32),
            jax.ShapeDtypeStruct(coupling.shape, jnp.float32),
        ),
        in_specs=[pl.BlockSpec(memory_space=pltpu.SMEM), vmem, vmem, vmem],
        out_specs=(vmem, vmem),
        name="finish_diagonals",
    )(order, sums, diag_inverse, coupling)


def shift(value, stride):
    count = lax.axis_size("row")
    return lax.ppermute(
        value, "row", [(at, at + stride) for at in range(count) if 0 <= at + stride < count]
    )


def swap(value, axis):
    return lax.ppermute(value, axis, [(at, at ^ 1) for at in range(lax.axis_size(axis))])


def pick(values, index):
    return lax.dynamic_index_in_dim(values, index, 0, keepdims=False)


def sum_devices(layout, sums, row, col):
    lines, line, side = layout.lines, row // 2, row % 2
    parts = sums.reshape(2, 2, lines, -1, layout.block)
    mine = pick(parts, col) + swap(pick(parts, 1 - col), "col")
    mine = pick(mine, side) + swap(pick(mine, 1 - side), "row")

    def turn(value, by):
        route = [
            (2 * at + side, 2 * ((at + by) % lines) + side)
            for at in range(lines)
            for side in range(2)
        ]
        return lax.ppermute(value, "row", route)

    came = [turn(pick(mine, (line + by) % lines), by) for by in range(1, lines)]
    share = sum(came, pick(mine, line))
    others = [share] + [turn(share, by) for by in range(1, lines)]
    stacked = jnp.stack(others)
    whole = jnp.zeros_like(stacked)
    for by in range(lines):
        whole = lax.dynamic_update_index_in_dim(whole, others[by], (line - by) % lines, 0)
    far = swap(whole, "row")
    sides = jnp.stack([jnp.where(side == 0, whole, far), jnp.where(side == 0, far, whole)])
    beside = swap(sides, "col")
    trees = jnp.stack([jnp.where(col == 0, sides, beside), jnp.where(col == 0, beside, sides)])
    return trees.reshape(sums.shape)


def live_units(ancestor_inverse, factor_panels, diag_inverse, coupling, block_pattern, tree_order):
    layout = Layout(
        lax.axis_size("row"), lax.axis_size("col"), ancestor_inverse.shape, factor_panels.shape
    )
    row, col = lax.axis_index("row"), lax.axis_index("col")
    place = jnp.stack([row, col]).astype(jnp.int32)
    line = row // 2
    plan = make_plan(layout, row, col, block_pattern, tree_order)
    units = compact_units(layout, plan, tree_order, factor_panels)

    def gather_and_multiply(room, units):
        own = lax.slice_in_dim(units, 0, room, axis=0)
        arrived = {(0, 0): own}
        half = room // 2

        def multiplied(total, buffers, first):
            which = list(range(first, first + len(buffers)))
            return gemm_units(layout, plan, place, total, ancestor_inverse, buffers, which)

        def phase(right, left, over, total, buffers, first):
            came = shift(right, 2), shift(left, -2), swap(over, "row")
            total = multiplied(total, buffers, first)
            return lax.optimization_barrier((came, total))

        def inward(values):
            return jnp.where(line < LINES // 2, values[1], values[0])

        first, total = phase(own, own, own, None, [own], 0)
        right = jnp.where(line == 0, first[2], first[0])
        left = jnp.where(line == LINES - 1, first[2], first[1])
        second, total = phase(right, left, inward(first), total, list(first), 1)
        third, total = phase(second[0], second[1], inward(second), total, list(second), 4)
        rest = lax.slice_in_dim(third[2], room - half, room, axis=0)
        over = lax.slice_in_dim(inward(third), 0, room - half, axis=0)
        last, total = phase(rest, rest, over, total, list(third), 7)
        fourth = jnp.concatenate([last[2], inward(last)])
        total = multiplied(total, [fourth], 10)
        buffers = [own, *first, *second, *third, fourth]
        other = swap(total, "col")
        return finish_columns(layout, plan, place, tree_order, total, other, coupling, buffers)

    most = plan[layout.most]
    rooms = sorted({-(-layout.units * part // 24) for part in (15, 16, 17, 18, 19, 20, 22, 24)})
    choice = sum((most > room).astype(jnp.int32) for room in rooms[:-1])
    branches = [functools.partial(gather_and_multiply, room) for room in rooms]
    inverse_panels, sums = lax.switch(choice, branches, units)
    sums = sum_devices(layout, sums, row, col)
    inverse_diagonal, inverse_coupling = finish_diagonals(tree_order, sums, diag_inverse, coupling)
    return inverse_panels, inverse_diagonal, inverse_coupling


def swapped(block, axis, bit):
    count = lax.axis_size(axis)
    route = []
    for low in range(count):
        high = low | 1 << bit
        if high != low and high < count:
            route += [(low, high), (high, low)]
    return lax.ppermute(block, axis, route)


def row_masks(pattern_eff, first_row, row_count, block_rows):
    row_index = first_row + jnp.arange(row_count, dtype=jnp.int32)
    blocks = row_index // block_rows
    onehot = (blocks[:, None] == jnp.arange(pattern_eff.shape[1], dtype=jnp.int32)[None, :]).astype(
        jnp.float32
    )
    return matmul(pattern_eff, onehot.T)


def whole_panels(ancestor_inverse, factor_panels, diag_inverse, coupling, block_pattern, tree_order):
    grid_row = lax.axis_index("row")
    grid_col = lax.axis_index("col")
    tile_rows = ancestor_inverse.shape[1]
    half_rows = ancestor_inverse.shape[2]
    piece_rows = factor_panels.shape[2]
    block_rows = factor_panels.shape[3]
    super_count = factor_panels.shape[0]
    share_rows = tile_rows // 2
    sorted_pattern = jnp.take(block_pattern, tree_order, axis=0).astype(jnp.float32)
    pattern_eff = jnp.concatenate(
        [sorted_pattern[:2], sorted_pattern[2:] * sorted_pattern[:2]], axis=0
    )
    source_mask = row_masks(
        pattern_eff, grid_col * half_rows + grid_row * piece_rows, piece_rows, block_rows
    )
    target_mask = row_masks(pattern_eff, grid_row * tile_rows, tile_rows, block_rows)
    panels = jnp.take(factor_panels, tree_order, axis=0) * source_mask[:, None, :, None]
    diag_blocks = jnp.take(diag_inverse, tree_order, axis=0)
    columns = []
    products = []
    for tree_slot in range(super_count):
        gathered = lax.all_gather(panels[tree_slot], "row", axis=1, tiled=True)
        columns.append(gathered)
        products.append(lax.psum(multiply(ancestor_inverse, gathered), "col"))
    own_flag = (grid_row * tile_rows // half_rows == grid_col).astype(jnp.float32)
    offset = jnp.clip(grid_row * tile_rows - grid_col * half_rows, 0, half_rows - tile_rows)
    own_windows = jnp.stack(
        [
            lax.dynamic_slice_in_dim(column_set, offset, tile_rows, 1) * own_flag
            for column_set in columns
        ]
    )
    partner_windows = swapped(own_windows, "col", 0)
    tile_windows = own_windows + partner_windows

    def share(matrix):
        return lax.dynamic_slice_in_dim(matrix, grid_col * share_rows, share_rows, 1)

    windows = [share(tile_windows[tree_slot]) for tree_slot in range(super_count)]
    parent_cols = [
        -target_mask[tree_slot][None, :, None] * products[tree_slot] for tree_slot in range(2)
    ]
    child_cols = [
        -target_mask[tree_slot + 2][None, :, None]
        * (products[tree_slot + 2] + multiply(parent_cols[tree_slot], coupling[tree_slot]))
        for tree_slot in range(2)
    ]
    parent_local = [
        multiply(flipped(windows[tree_slot]), share(parent_cols[tree_slot]))
        for tree_slot in range(2)
    ]
    cross_local = [
        multiply(flipped(share(parent_cols[tree_slot])), windows[tree_slot + 2])
        for tree_slot in range(2)
    ]
    child_local = [
        multiply(flipped(windows[tree_slot + 2]), share(child_cols[tree_slot]))
        for tree_slot in range(2)
    ]
    parent_sums = lax.psum(jnp.stack(parent_local), ("row", "col"))
    parent_diag = [diag_blocks[tree_slot] - parent_sums[tree_slot] for tree_slot in range(2)]
    child_totals = lax.psum(jnp.stack(cross_local + child_local), ("row", "col"))
    crosses = [
        -(child_totals[tree_slot] + multiply(parent_diag[tree_slot], coupling[tree_slot]))
        for tree_slot in range(2)
    ]
    child_sums = [child_totals[2 + tree_slot] for tree_slot in range(2)]
    child_diag = [
        diag_blocks[tree_slot + 2]
        - child_sums[tree_slot]
        - multiply(flipped(coupling[tree_slot]), crosses[tree_slot])
        for tree_slot in range(2)
    ]
    all_cols = jnp.stack(parent_cols + child_cols)
    all_diag = jnp.stack(parent_diag + child_diag)
    inverse_panels = jnp.zeros_like(all_cols).at[tree_order].set(all_cols)
    inverse_diagonal = jnp.zeros_like(all_diag).at[tree_order].set(all_diag)
    return (inverse_panels, inverse_diagonal, jnp.stack(crosses))


def per_device(ancestor_inverse, factor_panels, *others):
    row_count, col_count = lax.axis_size("row"), lax.axis_size("col")
    piece_rows, block = factor_panels.shape[2:]
    tile_rows, half_rows = ancestor_inverse.shape[1:]
    whole_blocks = piece_rows % block == 0 and half_rows % tile_rows == 0
    even_shares = row_count == 2 * LINES and 3 * block % LINES == 0
    if whole_blocks and col_count == 2 and even_shares:
        return live_units(ancestor_inverse, factor_panels, *others)
    return whole_panels(ancestor_inverse, factor_panels, *others)


def solution(mesh):
    return jax.shard_map(
        per_device,
        mesh=mesh,
        in_specs=(
            P(None, ("pole", "row"), "col"),
            P(None, None, ("pole", "col", "row"), None),
            P("pole", None, None, None),
            P("pole", None, None, None),
            P(),
            P(),
        ),
        out_specs=(
            P(None, None, ("pole", "row"), None),
            P("pole", None, None, None),
            P("pole", None, None, None),
        ),
        check_vma=False,
    )
```

```python
import functools

import jax
import jax.numpy as jnp
from jax import lax
from jax.experimental import pallas as pl
from jax.experimental.pallas import tpu as pltpu
from jax.sharding import PartitionSpec as P


def matmul(left_side, right_side):
    return jnp.dot(
        left_side, right_side, preferred_element_type=jnp.float32, precision=lax.Precision.HIGHEST
    )


def multiply(left_side, right_side):
    real_part = matmul(left_side[0], right_side[0]) - matmul(left_side[1], right_side[1])
    imag_part = matmul(left_side[0], right_side[1]) + matmul(left_side[1], right_side[0])
    return jnp.stack([real_part, imag_part])


def flipped(matrix):
    return jnp.swapaxes(matrix, 1, 2)


def halves(value):
    high = value.astype(jnp.bfloat16)
    low = (value - high.astype(jnp.float32)).astype(jnp.bfloat16)
    return high, low


def dot32(left_side, right_side, contract=((1,), (0,))):
    return lax.dot_general(
        left_side, right_side, (contract, ((), ())), preferred_element_type=jnp.float32
    )


def dot3(left_side, right_side, contract=((1,), (0,))):
    return (
        dot32(left_side[0], right_side[0], contract)
        + dot32(left_side[0], right_side[1], contract)
        + dot32(left_side[1], right_side[0], contract)
    )


ARRIVALS = (
    ("own", False, (0, 1, 2, 3)),
    ("right 1", False, (None, 0, 1, 2)),
    ("left 1", False, (1, 2, 3, None)),
    ("over 1", True, (0, 1, 2, 3)),
    ("right 2", (False, True, False, False), (None, 0, 0, 1)),
    ("left 2", (False, False, True, False), (2, 3, 3, None)),
    ("over 2", True, (1, 2, 1, 2)),
    ("right 3", False, (None, None, None, 0)),
    ("left 3", False, (3, None, None, None)),
    ("over 3", True, (2, 3, 0, 1)),
    ("over 4", True, (3, None, None, 0)),
)
LINES = len(ARRIVALS[0][2])


class Layout:
    def __init__(self, rows, cols, a_shape, p_shape):
        self.rows, self.cols = rows, cols
        self.lines = rows // 2
        self.slots, _, self.piece_rows, self.block = p_shape
        self.tile_rows, self.half_rows = a_shape[1:]
        self.piece_blocks = self.piece_rows // self.block
        self.tile_blocks = self.tile_rows // self.block
        self.half_blocks = self.half_rows // self.block
        self.units = self.piece_blocks * self.slots
        self.room = self.units - self.units // 6
        self.spare = self.units - self.room
        self.buffers = len(ARRIVALS)
        self.group = next(size for size in (4, 3, 2, 1) if self.tile_blocks % size == 0)
        self.ranks = 0
        self.source = cols * rows * self.units
        self.order = self.source + self.units
        self.live = self.order + self.slots * self.tile_blocks
        self.owners = self.live + self.slots
        self.windows = self.owners + self.buffers
        self.most = self.windows + 2
        self.total = self.most + 1


def plan_kernel(layout, place, pattern, order, plan):
    row, col = place[0], place[1]
    trees = layout.slots // 2
    names = [order[slot] for slot in range(layout.slots)]

    def live(slot, block):
        value = pattern[names[slot], block]
        if slot >= trees:
            value = value * pattern[names[slot - trees], block]
        return value

    def of_owner(owner, most):
        count = jnp.int32(0)
        for piece in range(layout.piece_blocks):
            for slot in range(layout.slots):
                value = live(slot, owner * layout.piece_blocks + piece)
                at = owner * layout.units + piece * layout.slots + slot
                plan[layout.ranks + at] = jnp.where(value > 0, count, -1)
                count = count + value
        return jnp.maximum(most, count)

    plan[layout.most] = lax.fori_loop(0, layout.cols * layout.rows, of_owner, jnp.int32(0))
    for unit in range(layout.units):
        plan[layout.source + unit] = 0
    mine = (col * layout.rows + row) * layout.units
    for unit in range(layout.units):
        rank = plan[layout.ranks + mine + unit]

        @pl.when(rank >= 0)
        def _():
            plan[layout.source + rank] = unit

    for slot in range(layout.slots):
        count = jnp.int32(0)
        values = []
        for index in range(layout.tile_blocks):
            value = live(slot, row * layout.tile_blocks + index)
            values.append(value)
            count = count + value
        plan[layout.live + slot] = count
        front, back = jnp.int32(0), count
        for index, value in enumerate(values):
            at = layout.order + slot * layout.tile_blocks + jnp.where(value > 0, front, back)
            plan[at] = index
            front, back = front + value, back + 1 - value

    line, side = row // 2, row % 2
    window_line = (row * layout.tile_blocks % layout.half_blocks) // layout.piece_blocks // 2
    windows = [jnp.int32(0), jnp.int32(0)]
    for index, (_, across, origins) in enumerate(ARRIVALS):
        owner = jnp.int32(-1)
        for at, origin in enumerate(origins):
            if origin is not None:
                crossed = across if isinstance(across, bool) else across[at]
                from_side = 1 - side if crossed else side
                owner = jnp.where(line == at, origin * 2 + from_side, owner)
        plan[layout.owners + index] = owner
        for which in range(2):
            hit = owner == window_line * 2 + which
            windows[which] = jnp.where(hit, index, windows[which])
    for which in range(2):
        plan[layout.windows + which] = windows[which]


def make_plan(layout, row, col, block_pattern, tree_order):
    smem = pl.BlockSpec(memory_space=pltpu.SMEM)
    return pl.pallas_call(
        functools.partial(plan_kernel, layout),
        out_shape=jax.ShapeDtypeStruct((layout.total,), jnp.int32),
        in_specs=[smem] * 3,
        out_specs=smem,
        name="make_plan",
    )(jnp.stack([row, col]).astype(jnp.int32), block_pattern, tree_order)


def compact_kernel(layout, plan, order, panels, units, spare, sems):
    block = layout.block
    copies = []
    for unit in range(layout.units):
        source = plan[layout.source + unit]
        first = pl.multiple_of(source // layout.slots * block, block)
        inside = unit < layout.room
        copy = pltpu.make_async_copy(
            panels.at[order[source % layout.slots], :, pl.ds(first, block), :],
            units.at[unit] if inside else spare.at[unit - layout.room],
            sems.at[unit],
        )
        copy.start()
        copies.append(copy)
    for copy in copies:
        copy.wait()


def compact_units(layout, plan, tree_order, panels):
    shapes = [(count, 2, layout.block, layout.block) for count in (layout.room, layout.spare)]
    return pl.pallas_call(
        functools.partial(compact_kernel, layout),
        out_shape=[jax.ShapeDtypeStruct(shape, jnp.float32) for shape in shapes],
        grid_spec=pltpu.PrefetchScalarGridSpec(
            num_scalar_prefetch=2,
            grid=(1,),
            in_specs=[pl.BlockSpec(memory_space=pltpu.HBM)],
            out_specs=[pl.BlockSpec(shape, lambda step, *_: (0, 0, 0, 0)) for shape in shapes],
            scratch_shapes=[pltpu.SemaphoreType.DMA((layout.units,))],
        ),
        compiler_params=pltpu.CompilerParams(vmem_limit_bytes=16 * 2**20),
        name="compact_units",
    )(plan, tree_order, panels)


def owner_at(layout, which, plan, step):
    if which is None:
        return step // layout.piece_blocks
    owner = plan[layout.owners + which[0]]
    for local in range(1, len(which)):
        later = step // layout.piece_blocks >= local
        owner = jnp.where(later, plan[layout.owners + which[local]], owner)
    return owner


def gemm_kernel(layout, which, parted, first_call, plan, place, *refs):
    refs = list(refs)
    in_ref = None if first_call else refs.pop(0)
    a_ref = refs.pop(0)
    *units, out_ref, total, weights, sem = refs
    step = pl.program_id(0)
    block, group = layout.block, layout.group
    width = 2 * block

    @pl.when(step == 0)
    def _():
        if first_call:
            total[...] = jnp.zeros_like(total)
        else:
            load = pltpu.make_async_copy(in_ref, total, sem)
            load.start()
            load.wait()

    owner = owner_at(layout, which, plan, step)
    base = place[1] * layout.rows * layout.units + owner * layout.units
    base = base + step % layout.piece_blocks * layout.slots
    front = units[0].shape[0]

    def places(rank):
        if which is None:
            return [(rank >= layout.room, lambda: units[0].at[owner, rank - layout.room])]
        if parted:
            lower = place[0] // 2 < LINES // 2
            inside, outside = (rank >= 0) & (rank < front), (rank >= front) & (rank < layout.room)
            return [
                (inside, lambda: units[0].at[rank]),
                (outside & ~lower, lambda: units[1].at[rank - front]),
                (outside & lower, lambda: units[2].at[rank - front]),
            ]
        inside = (rank >= 0) & (rank < layout.room)
        found = []
        for local, ref in enumerate(units):
            here = inside & (step // layout.piece_blocks == local)
            found.append((here, lambda ref=ref: ref.at[rank]))
        return found

    @pl.loop(0, jnp.where(owner >= 0, layout.slots, 0))
    def _(slot):
        rank = plan[layout.ranks + base + slot]
        if which is None:
            wanted = rank >= layout.room
        else:
            wanted = (rank >= 0) & (rank < layout.room)

        for here, find in places(rank):

            @pl.when(here)
            def _():
                unit = find()
                real, imag = unit[0], unit[1]
                real_parts, imag_parts = halves(real), halves(imag)
                for third, part in enumerate((0, 0, 1)):
                    top = third * width
                    weights[top : top + block, :block] = real_parts[part]
                    weights[top : top + block, block:] = imag_parts[part]
                    weights[top + block : top + width, :block] = -imag_parts[part]
                    weights[top + block : top + width, block:] = real_parts[part]

        alive = plan[layout.live + slot]

        @pl.loop(0, jnp.where(wanted, (alive + group - 1) // group, 0))
        def _(index):
            spans, lefts = [], []
            for at in range(group):
                first = plan[layout.order + slot * layout.tile_blocks + index * group + at]
                span = pl.ds(pl.multiple_of(first * block, block), block)
                real_high, real_low = halves(a_ref[0, span, :])
                imag_high, imag_low = halves(a_ref[1, span, :])
                spans.append(span)
                lefts.append(
                    jnp.concatenate(
                        [real_high, imag_high, real_low, imag_low, real_high, imag_high], axis=1
                    )
                )
            product = dot32(jnp.concatenate(lefts, axis=0), weights[...])
            for at, span in enumerate(spans):
                total[slot, span, :] += product[at * block : (at + 1) * block]

    @pl.when(step == pl.num_programs(0) - 1)
    def _():
        store = pltpu.make_async_copy(total, out_ref, sem)
        store.start()
        store.wait()


def gemm_units(layout, plan, place, total, ancestor_inverse, buffers, which, parted=False):
    first_call = total is None
    totals = [] if first_call else [total]
    hbm = pl.BlockSpec(memory_space=pltpu.HBM)
    block, pieces = layout.block, layout.piece_blocks
    rows, width = layout.tile_rows, 2 * layout.block

    def column(step, plan, place):
        owner = owner_at(layout, which, plan, step)
        return 0, 0, jnp.where(owner >= 0, owner * pieces + step % pieces, 0)

    shape = (layout.slots, rows, width)
    steps = (layout.rows if which is None else len(which)) * pieces
    return pl.pallas_call(
        functools.partial(gemm_kernel, layout, which, parted, first_call),
        out_shape=jax.ShapeDtypeStruct(shape, jnp.float32),
        grid_spec=pltpu.PrefetchScalarGridSpec(
            num_scalar_prefetch=2,
            grid=(steps,),
            in_specs=[hbm] * len(totals)
            + [pl.BlockSpec((2, rows, block), column)]
            + [
                pl.BlockSpec(
                    buffer.shape,
                    lambda step, plan, place, rank=buffer.ndim: (0,) * rank,
                    pipeline_mode=pl.Buffered(1),
                )
                for buffer in buffers
            ],
            out_specs=hbm,
            scratch_shapes=[
                pltpu.VMEM(shape, jnp.float32),
                pltpu.VMEM((3 * width, width), jnp.bfloat16),
                pltpu.SemaphoreType.DMA,
            ],
        ),
        input_output_aliases={} if first_call else {2: 0},
        compiler_params=pltpu.CompilerParams(vmem_limit_bytes=30 * 2**20),
        cost_estimate=pl.CostEstimate(
            flops=steps * layout.slots * 3 * 2 * rows * width * width // 2,
            bytes_accessed=steps * rows * block * 8 + 8 * layout.slots * rows * width,
            transcendentals=0,
        ),
        name="gemm_units",
    )(plan, place, *totals, ancestor_inverse, *buffers)


def window_kernel(layout, plan, place, *refs):
    buffers, (spare, out, sems) = refs[: layout.buffers - 1], refs[layout.buffers - 1 :]
    row, col = place[0], place[1]
    holds = row * layout.tile_blocks // layout.half_blocks == col
    owner = row * layout.tile_blocks % layout.half_blocks // layout.piece_blocks
    beyond = plan[layout.most] > layout.room

    def fetch(which, index):
        target = out.at[which, pl.ds(0, layout.room)]
        return pltpu.make_async_copy(buffers[index], target, sems.at[which])

    def fetch_spare(which):
        target = out.at[which, pl.ds(layout.room, layout.spare)]
        return pltpu.make_async_copy(spare.at[owner + which], target, sems.at[2 + which])

    for act in ("start", "wait"):
        for which in range(2):
            for index in range(layout.buffers - 1):

                @pl.when(holds & (plan[layout.windows + which] == index))
                def _():
                    getattr(fetch(which, index), act)()

            @pl.when(holds & beyond)
            def _():
                getattr(fetch_spare(which), act)()


def find_windows(layout, plan, place, buffers, spare):
    shape = (2, layout.units, 2, layout.block, layout.block)
    return pl.pallas_call(
        functools.partial(window_kernel, layout),
        out_shape=jax.ShapeDtypeStruct(shape, jnp.float32),
        grid_spec=pltpu.PrefetchScalarGridSpec(
            num_scalar_prefetch=2,
            grid=(1,),
            in_specs=[pl.BlockSpec(memory_space=pl.ANY)] * layout.buffers,
            out_specs=pl.BlockSpec(shape, lambda step, *_: (0, 0, 0, 0, 0)),
            scratch_shapes=[pltpu.SemaphoreType.DMA((4,))],
        ),
        compiler_params=pltpu.CompilerParams(vmem_limit_bytes=16 * 2**20),
        name="find_windows",
    )(plan, place, *buffers, spare)


def contract_kernel(layout, step_blocks, plan, place, mine, near, far, sums, acc, held, sem):
    step = pl.program_id(0)
    block, slots, trees = layout.block, layout.slots, layout.slots // 2
    row, col = place[0], place[1]
    half = row * layout.tile_blocks // layout.half_blocks
    inner = row * layout.tile_blocks % layout.half_blocks
    base = half * layout.rows * layout.units + inner * slots

    @pl.when(step == 0)
    def _():
        acc[...] = jnp.zeros_like(acc)
        for source, here in ((near, half == col), (far, half != col)):

            @pl.when(here)
            def _():
                copy = pltpu.make_async_copy(source, held, sem)
                copy.start()
                copy.wait()

    def window(slot):
        parts = []
        for at in range(step_blocks):
            index = step * step_blocks + at
            rank = plan[layout.ranks + base + index * slots + slot]
            unit = held.at[index // layout.piece_blocks, jnp.maximum(rank, 0)]
            whole = jnp.concatenate([unit[0], unit[1]], axis=1)
            parts.append(jnp.where(rank >= 0, -whole, 0.0))
        return halves(jnp.concatenate(parts, axis=0))

    rows_first = ((0,), (0,))

    @pl.loop(0, trees)
    def _(tree):
        child = tree + trees
        parent_parts = halves(mine[tree])
        child_panel = window(child)
        acc[3 * tree] += dot3(window(tree), parent_parts, rows_first)
        acc[3 * tree + 1] += dot3(child_panel, parent_parts, rows_first)
        acc[3 * tree + 2] += dot3(child_panel, halves(mine[child]), rows_first)

    @pl.when(step == pl.num_programs(0) - 1)
    def _():
        for index in range(3 * trees):
            value = acc[index]
            sums[index, 0] = value[:block, :block] - value[block:, block:]
            sums[index, 1] = value[:block, block:] + value[block:, :block]


def contract_windows(layout, plan, place, mine, near, far):
    block, slots = layout.block, layout.slots
    rows, width = layout.tile_rows, 2 * layout.block
    step_blocks = 2 if layout.piece_blocks % 2 == 0 else 1
    step_rows = step_blocks * block
    sums_shape = (3 * slots // 2, 2, block, block)
    return pl.pallas_call(
        functools.partial(contract_kernel, layout, step_blocks),
        out_shape=jax.ShapeDtypeStruct(sums_shape, jnp.float32),
        grid_spec=pltpu.PrefetchScalarGridSpec(
            num_scalar_prefetch=2,
            grid=(rows // step_rows,),
            in_specs=[pl.BlockSpec((slots, step_rows, width), lambda step, *_: (0, step, 0))]
            + [pl.BlockSpec(memory_space=pl.ANY)] * 2,
            out_specs=pl.BlockSpec(sums_shape, lambda step, *_: (0, 0, 0, 0)),
            scratch_shapes=[
                pltpu.VMEM((3 * slots // 2, width, width), jnp.float32),
                pltpu.VMEM(near.shape, jnp.float32),
                pltpu.SemaphoreType.DMA,
            ],
        ),
        compiler_params=pltpu.CompilerParams(vmem_limit_bytes=24 * 2**20),
        name="contract_windows",
    )(plan, place, mine, near, far)


def column_kernel(layout, step_blocks, first_step, plan, order, mine, other, coupling, *refs):
    step = pl.program_id(0) + first_step
    block, trees = layout.block, layout.slots // 2
    columns = refs[-1]

    def masked(slot, value):
        parts = []
        for at in range(step_blocks):
            alive = is_live(slot, step * step_blocks + at)
            parts.append(jnp.where(alive, -value[at * block : (at + 1) * block], 0.0))
        return jnp.concatenate(parts, axis=0)

    def is_live(slot, index):
        alive = jnp.bool_(False)
        for at in range(layout.tile_blocks):
            found = plan[layout.order + slot * layout.tile_blocks + at] == index
            alive = alive | (found & (at < plan[layout.live + slot]))
        return alive

    def put(slot, value):
        columns[order[slot], 0] = value[:, :block]
        columns[order[slot], 1] = value[:, block:]

    @pl.loop(0, trees)
    def _(tree):
        child = tree + trees
        real, imag = coupling[tree, 0], coupling[tree, 1]
        link = jnp.concatenate(
            [jnp.concatenate([real, imag], axis=1), jnp.concatenate([-imag, real], axis=1)], axis=0
        )
        parent_col = masked(tree, mine[tree] + other[tree])
        put(tree, parent_col)
        linked = dot3(halves(parent_col), halves(link))
        put(child, masked(child, mine[child] + other[child] + linked))


def finish_columns(layout, plan, tree_order, mine, other, coupling, begun=None):
    block, slots = layout.block, layout.slots
    rows, width = layout.tile_rows, 2 * layout.block
    step_blocks = 2 if layout.tile_blocks % 2 == 0 else 1
    step_rows = step_blocks * block
    steps = rows // step_rows
    first_step = 0 if begun is None else steps // 2
    count = steps // 2 if begun is None else steps - steps // 2
    half = pl.BlockSpec((slots, step_rows, width), lambda step, *_: (0, step + first_step, 0))
    return pl.pallas_call(
        functools.partial(column_kernel, layout, step_blocks, first_step),
        out_shape=jax.ShapeDtypeStruct((slots, 2, rows, block), jnp.float32),
        grid_spec=pltpu.PrefetchScalarGridSpec(
            num_scalar_prefetch=2,
            grid=(count,),
            in_specs=[half, half, pl.BlockSpec(coupling.shape, lambda step, *_: (0, 0, 0, 0))]
            + ([] if begun is None else [pl.BlockSpec(memory_space=pl.ANY)]),
            out_specs=pl.BlockSpec(
                (slots, 2, step_rows, block), lambda step, *_: (0, 0, step + first_step, 0)
            ),
        ),
        input_output_aliases={} if begun is None else {5: 0},
        compiler_params=pltpu.CompilerParams(vmem_limit_bytes=16 * 2**20),
        cost_estimate=pl.CostEstimate(
            flops=slots * 3 * rows * width * width // 2,
            bytes_accessed=6 * slots * rows * width,
            transcendentals=0,
        ),
        name="finish_columns",
    )(plan, tree_order, mine, other, coupling, *([] if begun is None else [begun]))


def complex_dot(left_side, right_side, contract=((1,), (0,))):
    def dot(left_part, right_part):
        return dot3(halves(left_side[left_part]), halves(right_side[right_part]), contract)

    return dot(0, 0) - dot(1, 1), dot(0, 1) + dot(1, 0)


def diagonal_kernel(order, sums, diag_in, coupling, diag_out, cross_out):
    trees = coupling.shape[0]
    for tree in range(trees):
        parent, child = order[tree], order[tree + trees]
        link = (coupling[tree, 0], coupling[tree, 1])
        parent_diag = tuple(diag_in[parent, part] - sums[3 * tree, part] for part in range(2))
        moved = complex_dot(parent_diag, link)
        between = tuple(sums[3 * tree + 1, part] for part in range(2))
        linked = complex_dot(between, link)
        cross = tuple(-(between[part].T + moved[part]) for part in range(2))
        back = complex_dot(link, cross, ((0,), (0,)))
        for part in range(2):
            diag_out[parent, part] = parent_diag[part]
            cross_out[tree, part] = cross[part]
            child_sum = sums[3 * tree + 2, part] - linked[part]
            diag_out[child, part] = diag_in[child, part] - child_sum - back[part]


def finish_diagonals(order, sums, diag_inverse, coupling):
    vmem = pl.BlockSpec(memory_space=pltpu.VMEM)
    return pl.pallas_call(
        diagonal_kernel,
        out_shape=(
            jax.ShapeDtypeStruct(diag_inverse.shape, jnp.float32),
            jax.ShapeDtypeStruct(coupling.shape, jnp.float32),
        ),
        in_specs=[pl.BlockSpec(memory_space=pltpu.SMEM), vmem, vmem, vmem],
        out_specs=(vmem, vmem),
        name="finish_diagonals",
    )(order, sums, diag_inverse, coupling)


def shift(value, stride):
    count = lax.axis_size("row")
    return lax.ppermute(
        value, "row", [(at, at + stride) for at in range(count) if 0 <= at + stride < count]
    )


def swap(value, axis):
    return lax.ppermute(value, axis, [(at, at ^ 1) for at in range(lax.axis_size(axis))])


def pick(values, index):
    return lax.dynamic_index_in_dim(values, index, 0, keepdims=False)


def sum_devices(layout, sums, row, col, begin, end):
    lines, line, side = layout.lines, row // 2, row % 2
    parts = sums.reshape(2, 2, lines, -1, layout.block)
    mine = pick(parts, col) + swap(pick(parts, 1 - col), "col")
    came, beside = lax.optimization_barrier((swap(pick(mine, 1 - side), "row"), begin()))
    mine = pick(mine, side) + came

    def turn(value, by):
        route = [
            (2 * at + side, 2 * ((at + by) % lines) + side)
            for at in range(lines)
            for side in range(2)
        ]
        return lax.ppermute(value, "row", route)

    came = [turn(pick(mine, (line + by) % lines), by) for by in range(1, lines)]
    came, beside = lax.optimization_barrier((came, end(beside)))
    share = sum(came, pick(mine, line))
    others = [share] + [turn(share, by) for by in range(1, lines)]
    stacked = jnp.stack(others)
    whole = jnp.zeros_like(stacked)
    for by in range(lines):
        whole = lax.dynamic_update_index_in_dim(whole, others[by], (line - by) % lines, 0)
    far = swap(whole, "row")
    sides = jnp.stack([jnp.where(side == 0, whole, far), jnp.where(side == 0, far, whole)])
    opposite = swap(sides, "col")
    trees = jnp.stack([jnp.where(col == 0, sides, opposite), jnp.where(col == 0, opposite, sides)])
    return trees.reshape(sums.shape), beside


def live_units(ancestor_inverse, factor_panels, diag_inverse, coupling, block_pattern, tree_order):
    layout = Layout(
        lax.axis_size("row"), lax.axis_size("col"), ancestor_inverse.shape, factor_panels.shape
    )
    row, col = lax.axis_index("row"), lax.axis_index("col")
    place = jnp.stack([row, col]).astype(jnp.int32)
    line = row // 2
    plan = make_plan(layout, row, col, block_pattern, tree_order)
    room = layout.room
    own, spare = compact_units(layout, plan, tree_order, factor_panels)
    half = room // 2

    def multiplied(total, buffers, first):
        which = None if first is None else list(range(first, first + len(buffers)))
        return gemm_units(layout, plan, place, total, ancestor_inverse, buffers, which)

    def phase(right, left, over, total, buffers, first):
        came = shift(right, 2), shift(left, -2), swap(over, "row")
        total = multiplied(total, buffers, first)
        return lax.optimization_barrier((came, total))

    def inward(values):
        return jnp.where(line < LINES // 2, values[1], values[0])

    first, total = phase(own, own, own, None, [own], 0)

    def beyond(_, state):
        gathered = lax.all_gather(spare, "row", axis=0, tiled=False)
        return gathered, multiplied(state[1], [gathered], None)

    trips = (plan[layout.most] > room).astype(jnp.int32)
    spares = jnp.zeros((layout.rows,) + spare.shape, jnp.float32)
    spares, total = lax.fori_loop(0, trips, beyond, (spares, total))

    right = jnp.where(line == 0, first[2], first[0])
    left = jnp.where(line == LINES - 1, first[2], first[1])
    second, total = phase(right, left, inward(first), total, list(first), 1)
    third, total = phase(second[0], second[1], inward(second), total, list(second), 4)
    rest = lax.slice_in_dim(third[2], room - half, room, axis=0)
    over = lax.slice_in_dim(inward(third), 0, room - half, axis=0)
    came = shift(rest, 2), shift(rest, -2), swap(over, "row")
    total = multiplied(total, list(third), 7)
    third, total = lax.optimization_barrier((third, total))
    near = find_windows(layout, plan, place, [own, *first, *second, *third], spares)
    far = swap(near, "col")
    last, total, near = lax.optimization_barrier((came, total, near))
    last = [last[2], last[0], last[1]]
    total = gemm_units(layout, plan, place, total, ancestor_inverse, last, [10], parted=True)

    other = swap(total, "col")
    sums = contract_windows(layout, plan, place, total, near, far)
    other, sums = lax.optimization_barrier((other, sums))
    columns = functools.partial(finish_columns, layout, plan, tree_order, total, other, coupling)
    sums, inverse_panels = sum_devices(layout, sums, row, col, columns, columns)
    inverse_diagonal, inverse_coupling = finish_diagonals(tree_order, sums, diag_inverse, coupling)
    return inverse_panels, inverse_diagonal, inverse_coupling


def swapped(block, axis, bit):
    count = lax.axis_size(axis)
    route = []
    for low in range(count):
        high = low | 1 << bit
        if high != low and high < count:
            route += [(low, high), (high, low)]
    return lax.ppermute(block, axis, route)


def row_masks(pattern_eff, first_row, row_count, block_rows):
    row_index = first_row + jnp.arange(row_count, dtype=jnp.int32)
    blocks = row_index // block_rows
    onehot = (blocks[:, None] == jnp.arange(pattern_eff.shape[1], dtype=jnp.int32)[None, :]).astype(
        jnp.float32
    )
    return matmul(pattern_eff, onehot.T)


def whole_panels(ancestor_inverse, factor_panels, diag_inverse, coupling, block_pattern, tree_order):
    grid_row = lax.axis_index("row")
    grid_col = lax.axis_index("col")
    tile_rows = ancestor_inverse.shape[1]
    half_rows = ancestor_inverse.shape[2]
    piece_rows = factor_panels.shape[2]
    block_rows = factor_panels.shape[3]
    super_count = factor_panels.shape[0]
    share_rows = tile_rows // 2
    sorted_pattern = jnp.take(block_pattern, tree_order, axis=0).astype(jnp.float32)
    pattern_eff = jnp.concatenate(
        [sorted_pattern[:2], sorted_pattern[2:] * sorted_pattern[:2]], axis=0
    )
    source_mask = row_masks(
        pattern_eff, grid_col * half_rows + grid_row * piece_rows, piece_rows, block_rows
    )
    target_mask = row_masks(pattern_eff, grid_row * tile_rows, tile_rows, block_rows)
    panels = jnp.take(factor_panels, tree_order, axis=0) * source_mask[:, None, :, None]
    diag_blocks = jnp.take(diag_inverse, tree_order, axis=0)
    columns = []
    products = []
    for tree_slot in range(super_count):
        gathered = lax.all_gather(panels[tree_slot], "row", axis=1, tiled=True)
        columns.append(gathered)
        products.append(lax.psum(multiply(ancestor_inverse, gathered), "col"))
    own_flag = (grid_row * tile_rows // half_rows == grid_col).astype(jnp.float32)
    offset = jnp.clip(grid_row * tile_rows - grid_col * half_rows, 0, half_rows - tile_rows)
    own_windows = jnp.stack(
        [
            lax.dynamic_slice_in_dim(column_set, offset, tile_rows, 1) * own_flag
            for column_set in columns
        ]
    )
    partner_windows = swapped(own_windows, "col", 0)
    tile_windows = own_windows + partner_windows

    def share(matrix):
        return lax.dynamic_slice_in_dim(matrix, grid_col * share_rows, share_rows, 1)

    windows = [share(tile_windows[tree_slot]) for tree_slot in range(super_count)]
    parent_cols = [
        -target_mask[tree_slot][None, :, None] * products[tree_slot] for tree_slot in range(2)
    ]
    child_cols = [
        -target_mask[tree_slot + 2][None, :, None]
        * (products[tree_slot + 2] + multiply(parent_cols[tree_slot], coupling[tree_slot]))
        for tree_slot in range(2)
    ]
    parent_local = [
        multiply(flipped(windows[tree_slot]), share(parent_cols[tree_slot]))
        for tree_slot in range(2)
    ]
    cross_local = [
        multiply(flipped(share(parent_cols[tree_slot])), windows[tree_slot + 2])
        for tree_slot in range(2)
    ]
    child_local = [
        multiply(flipped(windows[tree_slot + 2]), share(child_cols[tree_slot]))
        for tree_slot in range(2)
    ]
    parent_sums = lax.psum(jnp.stack(parent_local), ("row", "col"))
    parent_diag = [diag_blocks[tree_slot] - parent_sums[tree_slot] for tree_slot in range(2)]
    child_totals = lax.psum(jnp.stack(cross_local + child_local), ("row", "col"))
    crosses = [
        -(child_totals[tree_slot] + multiply(parent_diag[tree_slot], coupling[tree_slot]))
        for tree_slot in range(2)
    ]
    child_sums = [child_totals[2 + tree_slot] for tree_slot in range(2)]
    child_diag = [
        diag_blocks[tree_slot + 2]
        - child_sums[tree_slot]
        - multiply(flipped(coupling[tree_slot]), crosses[tree_slot])
        for tree_slot in range(2)
    ]
    all_cols = jnp.stack(parent_cols + child_cols)
    all_diag = jnp.stack(parent_diag + child_diag)
    inverse_panels = jnp.zeros_like(all_cols).at[tree_order].set(all_cols)
    inverse_diagonal = jnp.zeros_like(all_diag).at[tree_order].set(all_diag)
    return (inverse_panels, inverse_diagonal, jnp.stack(crosses))


def per_device(ancestor_inverse, factor_panels, *others):
    row_count, col_count = lax.axis_size("row"), lax.axis_size("col")
    piece_rows, block = factor_panels.shape[2:]
    tile_rows, half_rows = ancestor_inverse.shape[1:]
    whole_blocks = piece_rows % block == 0 and half_rows % tile_rows == 0
    even_shares = row_count == 2 * LINES and 3 * block % LINES == 0
    if whole_blocks and col_count == 2 and even_shares:
        return live_units(ancestor_inverse, factor_panels, *others)
    return whole_panels(ancestor_inverse, factor_panels, *others)


def solution(mesh):
    return jax.shard_map(
        per_device,
        mesh=mesh,
        in_specs=(
            P(None, ("pole", "row"), "col"),
            P(None, None, ("pole", "col", "row"), None),
            P("pole", None, None, None),
            P("pole", None, None, None),
            P(),
            P(),
        ),
        out_specs=(
            P(None, None, ("pole", "row"), None),
            P("pole", None, None, None),
            P("pole", None, None, None),
        ),
        check_vma=False,
    )
```

```python
import functools

import jax
import jax.numpy as jnp
from jax import lax
from jax.experimental import pallas as pl
from jax.experimental.pallas import tpu as pltpu
from jax.sharding import PartitionSpec as P


def matmul(left_side, right_side):
    return jnp.dot(
        left_side, right_side, preferred_element_type=jnp.float32, precision=lax.Precision.HIGHEST
    )


def multiply(left_side, right_side):
    real_part = matmul(left_side[0], right_side[0]) - matmul(left_side[1], right_side[1])
    imag_part = matmul(left_side[0], right_side[1]) + matmul(left_side[1], right_side[0])
    return jnp.stack([real_part, imag_part])


def flipped(matrix):
    return jnp.swapaxes(matrix, 1, 2)


def halves(value):
    high = value.astype(jnp.bfloat16)
    low = (value - high.astype(jnp.float32)).astype(jnp.bfloat16)
    return high, low


def dot32(left_side, right_side, contract=((1,), (0,))):
    return lax.dot_general(
        left_side, right_side, (contract, ((), ())), preferred_element_type=jnp.float32
    )


def dot3(left_side, right_side, contract=((1,), (0,))):
    return (
        dot32(left_side[0], right_side[0], contract)
        + dot32(left_side[0], right_side[1], contract)
        + dot32(left_side[1], right_side[0], contract)
    )


ARRIVALS = (
    ("own", False, (0, 1, 2, 3)),
    ("right 1", False, (None, 0, 1, 2)),
    ("left 1", False, (1, 2, 3, None)),
    ("over 1", True, (0, 1, 2, 3)),
    ("right 2", False, (None, None, 0, 1)),
    ("left 2", False, (2, 3, None, None)),
    ("out 2", True, (None, 0, 3, None)),
    ("over 2", True, (1, 2, 1, 2)),
    ("right 3", False, (None, None, None, 0)),
    ("left 3", False, (3, None, None, None)),
    ("over 3", True, (2, 3, 0, 1)),
    ("over 4", True, (3, None, None, 0)),
)
LINES = len(ARRIVALS[0][2])


class Layout:
    def __init__(self, rows, cols, a_shape, p_shape):
        self.rows, self.cols = rows, cols
        self.lines = rows // 2
        self.slots, _, self.piece_rows, self.block = p_shape
        self.tile_rows, self.half_rows = a_shape[1:]
        self.piece_blocks = self.piece_rows // self.block
        self.tile_blocks = self.tile_rows // self.block
        self.half_blocks = self.half_rows // self.block
        self.units = self.piece_blocks * self.slots
        self.room = self.units - self.units // 6
        self.spare = self.units - self.room
        self.buffers = len(ARRIVALS)
        self.group = next(size for size in (4, 3, 2, 1) if self.tile_blocks % size == 0)
        self.ranks = 0
        self.source = cols * rows * self.units
        self.order = self.source + self.units
        self.live = self.order + self.slots * self.tile_blocks
        self.owners = self.live + self.slots
        self.windows = self.owners + self.buffers
        self.most = self.windows + 2
        self.total = self.most + 1


def plan_kernel(layout, place, pattern, order, plan):
    row, col = place[0], place[1]
    trees = layout.slots // 2
    names = [order[slot] for slot in range(layout.slots)]

    def live(slot, block):
        value = pattern[names[slot], block]
        if slot >= trees:
            value = value * pattern[names[slot - trees], block]
        return value

    def of_owner(owner, most):
        count = jnp.int32(0)
        for piece in range(layout.piece_blocks):
            for slot in range(layout.slots):
                value = live(slot, owner * layout.piece_blocks + piece)
                at = owner * layout.units + piece * layout.slots + slot
                plan[layout.ranks + at] = jnp.where(value > 0, count, -1)
                count = count + value
        return jnp.maximum(most, count)

    plan[layout.most] = lax.fori_loop(0, layout.cols * layout.rows, of_owner, jnp.int32(0))
    for unit in range(layout.units):
        plan[layout.source + unit] = 0
    mine = (col * layout.rows + row) * layout.units
    for unit in range(layout.units):
        rank = plan[layout.ranks + mine + unit]

        @pl.when(rank >= 0)
        def _():
            plan[layout.source + rank] = unit

    for slot in range(layout.slots):
        count = jnp.int32(0)
        values = []
        for index in range(layout.tile_blocks):
            value = live(slot, row * layout.tile_blocks + index)
            values.append(value)
            count = count + value
        plan[layout.live + slot] = count
        front, back = jnp.int32(0), count
        for index, value in enumerate(values):
            at = layout.order + slot * layout.tile_blocks + jnp.where(value > 0, front, back)
            plan[at] = index
            front, back = front + value, back + 1 - value

    line, side = row // 2, row % 2
    window_line = (row * layout.tile_blocks % layout.half_blocks) // layout.piece_blocks // 2
    windows = [jnp.int32(0), jnp.int32(0)]
    for index, (_, across, origins) in enumerate(ARRIVALS):
        owner = jnp.int32(-1)
        for at, origin in enumerate(origins):
            if origin is not None:
                from_side = 1 - side if across else side
                owner = jnp.where(line == at, origin * 2 + from_side, owner)
        plan[layout.owners + index] = owner
        for which in range(2):
            hit = owner == window_line * 2 + which
            windows[which] = jnp.where(hit, index, windows[which])
    for which in range(2):
        plan[layout.windows + which] = windows[which]


def make_plan(layout, row, col, block_pattern, tree_order):
    smem = pl.BlockSpec(memory_space=pltpu.SMEM)
    return pl.pallas_call(
        functools.partial(plan_kernel, layout),
        out_shape=jax.ShapeDtypeStruct((layout.total,), jnp.int32),
        in_specs=[smem] * 3,
        out_specs=smem,
        name="make_plan",
    )(jnp.stack([row, col]).astype(jnp.int32), block_pattern, tree_order)


def compact_kernel(layout, plan, order, panels, units, spare, sems):
    block = layout.block
    copies = []
    for unit in range(layout.units):
        source = plan[layout.source + unit]
        first = pl.multiple_of(source // layout.slots * block, block)
        inside = unit < layout.room
        copy = pltpu.make_async_copy(
            panels.at[order[source % layout.slots], :, pl.ds(first, block), :],
            units.at[unit] if inside else spare.at[unit - layout.room],
            sems.at[unit],
        )
        copy.start()
        copies.append(copy)
    for copy in copies:
        copy.wait()


def compact_units(layout, plan, tree_order, panels):
    shapes = [(count, 2, layout.block, layout.block) for count in (layout.room, layout.spare)]
    return pl.pallas_call(
        functools.partial(compact_kernel, layout),
        out_shape=[jax.ShapeDtypeStruct(shape, jnp.float32) for shape in shapes],
        grid_spec=pltpu.PrefetchScalarGridSpec(
            num_scalar_prefetch=2,
            grid=(1,),
            in_specs=[pl.BlockSpec(memory_space=pltpu.HBM)],
            out_specs=[pl.BlockSpec(shape, lambda step, *_: (0, 0, 0, 0)) for shape in shapes],
            scratch_shapes=[pltpu.SemaphoreType.DMA((layout.units,))],
        ),
        compiler_params=pltpu.CompilerParams(vmem_limit_bytes=16 * 2**20),
        name="compact_units",
    )(plan, tree_order, panels)


def owner_at(layout, which, plan, step):
    if which is None:
        return step // layout.piece_blocks
    owner = plan[layout.owners + which[0]]
    for local in range(1, len(which)):
        later = step // layout.piece_blocks >= local
        owner = jnp.where(later, plan[layout.owners + which[local]], owner)
    return owner


def gemm_kernel(layout, which, parted, first_call, plan, place, *refs):
    refs = list(refs)
    in_ref = None if first_call else refs.pop(0)
    a_ref = refs.pop(0)
    *units, out_ref, total, a_parts, weights, sems = refs
    step = pl.program_id(0)
    block, rows = layout.block, layout.tile_rows
    width = 2 * block

    def each_slot(source, target, act):
        for slot in range(layout.slots):
            getattr(pltpu.make_async_copy(source.at[slot], target.at[slot], sems.at[slot]), act)()

    @pl.when(step == 0)
    def _():
        if first_call:
            total[...] = jnp.zeros_like(total)
        else:
            each_slot(in_ref, total, "start")

    owner = owner_at(layout, which, plan, step)

    @pl.loop(0, jnp.where(owner >= 0, rows // block, 0))
    def _(index):
        span = pl.ds(pl.multiple_of(index * block, block), block)
        for part in range(2):
            high, low = halves(a_ref[part, span, :])
            a_parts[span, part * block : (part + 1) * block] = high
            a_parts[span, width + part * block : width + (part + 1) * block] = low
            a_parts[span, 2 * width + part * block : 2 * width + (part + 1) * block] = high

    if not first_call:

        @pl.when(step == 0)
        def _():
            each_slot(in_ref, total, "wait")

    base = place[1] * layout.rows * layout.units + owner * layout.units
    base = base + step % layout.piece_blocks * layout.slots
    front = units[0].shape[0]

    def places(rank):
        if which is None:
            return [(rank >= layout.room, lambda: units[0].at[owner, rank - layout.room])]
        if parted:
            lower = place[0] // 2 < LINES // 2
            inside, outside = (rank >= 0) & (rank < front), (rank >= front) & (rank < layout.room)
            return [
                (inside, lambda: units[0].at[rank]),
                (outside & ~lower, lambda: units[1].at[rank - front]),
                (outside & lower, lambda: units[2].at[rank - front]),
            ]
        inside = (rank >= 0) & (rank < layout.room)
        found = []
        for local, ref in enumerate(units):
            here = inside & (step // layout.piece_blocks == local)
            found.append((here, lambda ref=ref: ref.at[rank]))
        return found

    @pl.loop(0, jnp.where(owner >= 0, layout.slots, 0))
    def _(slot):
        rank = plan[layout.ranks + base + slot]
        if which is None:
            wanted = rank >= layout.room
        else:
            wanted = (rank >= 0) & (rank < layout.room)

        for here, find in places(rank):

            @pl.when(here)
            def _():
                unit = find()
                real, imag = unit[0], unit[1]
                real_parts, imag_parts = halves(real), halves(imag)
                for third, part in enumerate((0, 0, 1)):
                    top = third * width
                    weights[top : top + block, :block] = real_parts[part]
                    weights[top : top + block, block:] = imag_parts[part]
                    weights[top + block : top + width, :block] = -imag_parts[part]
                    weights[top + block : top + width, block:] = real_parts[part]

        @pl.when(wanted & (plan[layout.live + slot] > 0))
        def _():
            total[slot] += dot32(a_parts[...], weights[...])

    @pl.when(step == pl.num_programs(0) - 1)
    def _():
        each_slot(total, out_ref, "start")
        each_slot(total, out_ref, "wait")


def gemm_units(layout, plan, place, total, ancestor_inverse, buffers, which, parted=False):
    first_call = total is None
    totals = [] if first_call else [total]
    hbm = pl.BlockSpec(memory_space=pltpu.HBM)
    block, pieces = layout.block, layout.piece_blocks
    rows, width = layout.tile_rows, 2 * layout.block

    def column(step, plan, place):
        owner = owner_at(layout, which, plan, step)
        return 0, 0, jnp.where(owner >= 0, owner * pieces + step % pieces, 0)

    shape = (layout.slots, rows, width)
    steps = (layout.rows if which is None else len(which)) * pieces
    return pl.pallas_call(
        functools.partial(gemm_kernel, layout, which, parted, first_call),
        out_shape=jax.ShapeDtypeStruct(shape, jnp.float32),
        grid_spec=pltpu.PrefetchScalarGridSpec(
            num_scalar_prefetch=2,
            grid=(steps,),
            in_specs=[hbm] * len(totals)
            + [pl.BlockSpec((2, rows, block), column)]
            + [
                pl.BlockSpec(
                    buffer.shape,
                    lambda step, plan, place, rank=buffer.ndim: (0,) * rank,
                    pipeline_mode=pl.Buffered(1),
                )
                for buffer in buffers
            ],
            out_specs=hbm,
            scratch_shapes=[
                pltpu.VMEM(shape, jnp.float32),
                pltpu.VMEM((rows, 3 * width), jnp.bfloat16),
                pltpu.VMEM((3 * width, width), jnp.bfloat16),
                pltpu.SemaphoreType.DMA((layout.slots,)),
            ],
        ),
        input_output_aliases={} if first_call else {2: 0},
        compiler_params=pltpu.CompilerParams(vmem_limit_bytes=36 * 2**20),
        cost_estimate=pl.CostEstimate(
            flops=steps * layout.slots * 3 * 2 * rows * width * width // 2,
            bytes_accessed=steps * rows * block * 8 + 8 * layout.slots * rows * width,
            transcendentals=0,
        ),
        name="gemm_units",
    )(plan, place, *totals, ancestor_inverse, *buffers)


def window_kernel(layout, plan, place, *refs):
    buffers, (spare, out, sems) = refs[: layout.buffers - 1], refs[layout.buffers - 1 :]
    row, col = place[0], place[1]
    holds = row * layout.tile_blocks // layout.half_blocks == col
    owner = row * layout.tile_blocks % layout.half_blocks // layout.piece_blocks
    beyond = plan[layout.most] > layout.room

    def fetch(which, index):
        target = out.at[which, pl.ds(0, layout.room)]
        return pltpu.make_async_copy(buffers[index], target, sems.at[which])

    def fetch_spare(which):
        target = out.at[which, pl.ds(layout.room, layout.spare)]
        return pltpu.make_async_copy(spare.at[owner + which], target, sems.at[2 + which])

    for act in ("start", "wait"):
        for which in range(2):
            for index in range(layout.buffers - 1):

                @pl.when(holds & (plan[layout.windows + which] == index))
                def _():
                    getattr(fetch(which, index), act)()

            @pl.when(holds & beyond)
            def _():
                getattr(fetch_spare(which), act)()


def find_windows(layout, plan, place, buffers, spare):
    shape = (2, layout.units, 2, layout.block, layout.block)
    return pl.pallas_call(
        functools.partial(window_kernel, layout),
        out_shape=jax.ShapeDtypeStruct(shape, jnp.float32),
        grid_spec=pltpu.PrefetchScalarGridSpec(
            num_scalar_prefetch=2,
            grid=(1,),
            in_specs=[pl.BlockSpec(memory_space=pl.ANY)] * layout.buffers,
            out_specs=pl.BlockSpec(shape, lambda step, *_: (0, 0, 0, 0, 0)),
            scratch_shapes=[pltpu.SemaphoreType.DMA((4,))],
        ),
        compiler_params=pltpu.CompilerParams(vmem_limit_bytes=16 * 2**20),
        name="find_windows",
    )(plan, place, *buffers, spare)


def contract_kernel(layout, step_blocks, plan, place, mine, near, far, sums, acc, held, sem):
    step = pl.program_id(0)
    block, slots, trees = layout.block, layout.slots, layout.slots // 2
    row, col = place[0], place[1]
    half = row * layout.tile_blocks // layout.half_blocks
    inner = row * layout.tile_blocks % layout.half_blocks
    base = half * layout.rows * layout.units + inner * slots

    @pl.when(step == 0)
    def _():
        acc[...] = jnp.zeros_like(acc)
        for source, here in ((near, half == col), (far, half != col)):

            @pl.when(here)
            def _():
                copy = pltpu.make_async_copy(source, held, sem)
                copy.start()
                copy.wait()

    def window(slot):
        parts = []
        for at in range(step_blocks):
            index = step * step_blocks + at
            rank = plan[layout.ranks + base + index * slots + slot]
            unit = held.at[index // layout.piece_blocks, jnp.maximum(rank, 0)]
            whole = jnp.concatenate([unit[0], unit[1]], axis=1)
            parts.append(jnp.where(rank >= 0, -whole, 0.0))
        return halves(jnp.concatenate(parts, axis=0))

    rows_first = ((0,), (0,))

    @pl.loop(0, trees)
    def _(tree):
        child = tree + trees
        parent_parts = halves(mine[tree])
        child_panel = window(child)
        acc[3 * tree] += dot3(window(tree), parent_parts, rows_first)
        acc[3 * tree + 1] += dot3(child_panel, parent_parts, rows_first)
        acc[3 * tree + 2] += dot3(child_panel, halves(mine[child]), rows_first)

    @pl.when(step == pl.num_programs(0) - 1)
    def _():
        for index in range(3 * trees):
            value = acc[index]
            sums[index, 0] = value[:block, :block] - value[block:, block:]
            sums[index, 1] = value[:block, block:] + value[block:, :block]


def contract_windows(layout, plan, place, mine, near, far):
    block, slots = layout.block, layout.slots
    rows, width = layout.tile_rows, 2 * layout.block
    step_blocks = layout.group
    step_rows = step_blocks * block
    sums_shape = (3 * slots // 2, 2, block, block)
    return pl.pallas_call(
        functools.partial(contract_kernel, layout, step_blocks),
        out_shape=jax.ShapeDtypeStruct(sums_shape, jnp.float32),
        grid_spec=pltpu.PrefetchScalarGridSpec(
            num_scalar_prefetch=2,
            grid=(rows // step_rows,),
            in_specs=[pl.BlockSpec((slots, step_rows, width), lambda step, *_: (0, step, 0))]
            + [pl.BlockSpec(memory_space=pl.ANY)] * 2,
            out_specs=pl.BlockSpec(sums_shape, lambda step, *_: (0, 0, 0, 0)),
            scratch_shapes=[
                pltpu.VMEM((3 * slots // 2, width, width), jnp.float32),
                pltpu.VMEM(near.shape, jnp.float32),
                pltpu.SemaphoreType.DMA,
            ],
        ),
        compiler_params=pltpu.CompilerParams(vmem_limit_bytes=24 * 2**20),
        name="contract_windows",
    )(plan, place, mine, near, far)


def column_kernel(layout, step_blocks, first_step, plan, order, mine, other, coupling, *refs):
    step = pl.program_id(0) + first_step
    block, trees = layout.block, layout.slots // 2
    columns = refs[-1]

    def masked(slot, value):
        parts = []
        for at in range(step_blocks):
            alive = is_live(slot, step * step_blocks + at)
            parts.append(jnp.where(alive, -value[at * block : (at + 1) * block], 0.0))
        return jnp.concatenate(parts, axis=0)

    def is_live(slot, index):
        alive = jnp.bool_(False)
        for at in range(layout.tile_blocks):
            found = plan[layout.order + slot * layout.tile_blocks + at] == index
            alive = alive | (found & (at < plan[layout.live + slot]))
        return alive

    def put(slot, value):
        columns[order[slot], 0] = value[:, :block]
        columns[order[slot], 1] = value[:, block:]

    @pl.loop(0, trees)
    def _(tree):
        child = tree + trees
        real, imag = coupling[tree, 0], coupling[tree, 1]
        link = jnp.concatenate(
            [jnp.concatenate([real, imag], axis=1), jnp.concatenate([-imag, real], axis=1)], axis=0
        )
        parent_col = masked(tree, mine[tree] + other[tree])
        put(tree, parent_col)
        linked = dot3(halves(parent_col), halves(link))
        put(child, masked(child, mine[child] + other[child] + linked))


def finish_columns(layout, plan, tree_order, mine, other, coupling, begun=None):
    block, slots = layout.block, layout.slots
    rows, width = layout.tile_rows, 2 * layout.block
    step_blocks = 2 if layout.tile_blocks % 2 == 0 else 1
    step_rows = step_blocks * block
    steps = rows // step_rows
    first_step = 0 if begun is None else steps // 2
    count = steps // 2 if begun is None else steps - steps // 2
    half = pl.BlockSpec((slots, step_rows, width), lambda step, *_: (0, step + first_step, 0))
    return pl.pallas_call(
        functools.partial(column_kernel, layout, step_blocks, first_step),
        out_shape=jax.ShapeDtypeStruct((slots, 2, rows, block), jnp.float32),
        grid_spec=pltpu.PrefetchScalarGridSpec(
            num_scalar_prefetch=2,
            grid=(count,),
            in_specs=[half, half, pl.BlockSpec(coupling.shape, lambda step, *_: (0, 0, 0, 0))]
            + ([] if begun is None else [pl.BlockSpec(memory_space=pl.ANY)]),
            out_specs=pl.BlockSpec(
                (slots, 2, step_rows, block), lambda step, *_: (0, 0, step + first_step, 0)
            ),
        ),
        input_output_aliases={} if begun is None else {5: 0},
        compiler_params=pltpu.CompilerParams(vmem_limit_bytes=16 * 2**20),
        cost_estimate=pl.CostEstimate(
            flops=slots * 3 * rows * width * width // 2,
            bytes_accessed=6 * slots * rows * width,
            transcendentals=0,
        ),
        name="finish_columns",
    )(plan, tree_order, mine, other, coupling, *([] if begun is None else [begun]))


def complex_dot(left_side, right_side, contract=((1,), (0,))):
    def dot(left_part, right_part):
        return dot3(halves(left_side[left_part]), halves(right_side[right_part]), contract)

    return dot(0, 0) - dot(1, 1), dot(0, 1) + dot(1, 0)


def diagonal_kernel(order, sums, diag_in, coupling, diag_out, cross_out):
    trees = coupling.shape[0]
    for tree in range(trees):
        parent, child = order[tree], order[tree + trees]
        link = (coupling[tree, 0], coupling[tree, 1])
        parent_diag = tuple(diag_in[parent, part] - sums[3 * tree, part] for part in range(2))
        moved = complex_dot(parent_diag, link)
        between = tuple(sums[3 * tree + 1, part] for part in range(2))
        linked = complex_dot(between, link)
        cross = tuple(-(between[part].T + moved[part]) for part in range(2))
        back = complex_dot(link, cross, ((0,), (0,)))
        for part in range(2):
            diag_out[parent, part] = parent_diag[part]
            cross_out[tree, part] = cross[part]
            child_sum = sums[3 * tree + 2, part] - linked[part]
            diag_out[child, part] = diag_in[child, part] - child_sum - back[part]


def finish_diagonals(order, sums, diag_inverse, coupling):
    vmem = pl.BlockSpec(memory_space=pltpu.VMEM)
    return pl.pallas_call(
        diagonal_kernel,
        out_shape=(
            jax.ShapeDtypeStruct(diag_inverse.shape, jnp.float32),
            jax.ShapeDtypeStruct(coupling.shape, jnp.float32),
        ),
        in_specs=[pl.BlockSpec(memory_space=pltpu.SMEM), vmem, vmem, vmem],
        out_specs=(vmem, vmem),
        name="finish_diagonals",
    )(order, sums, diag_inverse, coupling)


def along(value, lines, step):
    route = [(2 * at + side, 2 * (at + step) + side) for at in lines for side in range(2)]
    return lax.ppermute(value, "row", route)


def swap(value, axis):
    return lax.ppermute(value, axis, [(at, at ^ 1) for at in range(lax.axis_size(axis))])


def pick(values, index):
    return lax.dynamic_index_in_dim(values, index, 0, keepdims=False)


def sum_devices(layout, sums, row, col, begin, end):
    lines, line, side = layout.lines, row // 2, row % 2
    parts = sums.reshape(2, 2, lines, -1, layout.block)
    mine = pick(parts, col) + swap(pick(parts, 1 - col), "col")
    came, beside = lax.optimization_barrier((swap(pick(mine, 1 - side), "row"), begin()))
    mine = pick(mine, side) + came

    def turn(value, by):
        route = [
            (2 * at + side, 2 * ((at + by) % lines) + side)
            for at in range(lines)
            for side in range(2)
        ]
        return lax.ppermute(value, "row", route)

    came = [turn(pick(mine, (line + by) % lines), by) for by in range(1, lines)]
    came, beside = lax.optimization_barrier((came, end(beside)))
    share = sum(came, pick(mine, line))
    others = [share] + [turn(share, by) for by in range(1, lines)]
    stacked = jnp.stack(others)
    whole = jnp.zeros_like(stacked)
    for by in range(lines):
        whole = lax.dynamic_update_index_in_dim(whole, others[by], (line - by) % lines, 0)
    far = swap(whole, "row")
    sides = jnp.stack([jnp.where(side == 0, whole, far), jnp.where(side == 0, far, whole)])
    opposite = swap(sides, "col")
    trees = jnp.stack([jnp.where(col == 0, sides, opposite), jnp.where(col == 0, opposite, sides)])
    return trees.reshape(sums.shape), beside


def live_units(ancestor_inverse, factor_panels, diag_inverse, coupling, block_pattern, tree_order):
    layout = Layout(
        lax.axis_size("row"), lax.axis_size("col"), ancestor_inverse.shape, factor_panels.shape
    )
    row, col = lax.axis_index("row"), lax.axis_index("col")
    place = jnp.stack([row, col]).astype(jnp.int32)
    line = row // 2
    plan = make_plan(layout, row, col, block_pattern, tree_order)
    room = layout.room
    own, spare = compact_units(layout, plan, tree_order, factor_panels)
    half = room // 2

    def multiplied(total, buffers, first):
        which = None if first is None else list(range(first, first + len(buffers)))
        return gemm_units(layout, plan, place, total, ancestor_inverse, buffers, which)

    def phase(came, total, buffers, first):
        return lax.optimization_barrier((came, multiplied(total, buffers, first)))

    def inward(values):
        return jnp.where(line < LINES // 2, values[1], values[0])

    came = along(own, range(LINES - 1), 1), along(own, range(1, LINES), -1), swap(own, "row")
    first, total = phase(came, None, [own], 0)

    def beyond(_, state):
        gathered = lax.all_gather(spare, "row", axis=0, tiled=False)
        return gathered, multiplied(state[1], [gathered], None)

    trips = (plan[layout.most] > room).astype(jnp.int32)
    spares = jnp.zeros((layout.rows,) + spare.shape, jnp.float32)
    spares, total = lax.fori_loop(0, trips, beyond, (spares, total))

    end = LINES - 1
    came = along(first[0], range(1, end), 1), along(first[1], range(1, end), -1)
    outward = [(at, at + 2) for at in range(2)] + [(at + 2 * end, at + 2 * end - 2) for at in range(2)]
    came += lax.ppermute(first[2], "row", outward), swap(inward(first), "row")
    second, total = phase(came, total, list(first), 1)
    came = along(second[0], [end - 1], 1), along(second[1], [1], -1), swap(inward(second), "row")
    third, total = phase(came, total, list(second), 4)
    rest = lax.slice_in_dim(third[2], room - half, room, axis=0)
    over = lax.slice_in_dim(inward(third), 0, room - half, axis=0)
    came = along(rest, [end - 1], 1), along(rest, [1], -1), swap(over, "row")
    total = multiplied(total, list(third), 8)
    third, total = lax.optimization_barrier((third, total))
    near = find_windows(layout, plan, place, [own, *first, *second, *third], spares)
    far = swap(near, "col")
    last, total, near = lax.optimization_barrier((came, total, near))
    last = [last[2], last[0], last[1]]
    total = gemm_units(layout, plan, place, total, ancestor_inverse, last, [11], parted=True)

    other = swap(total, "col")
    sums = contract_windows(layout, plan, place, total, near, far)
    other, sums = lax.optimization_barrier((other, sums))
    columns = functools.partial(finish_columns, layout, plan, tree_order, total, other, coupling)
    sums, inverse_panels = sum_devices(layout, sums, row, col, columns, columns)
    inverse_diagonal, inverse_coupling = finish_diagonals(tree_order, sums, diag_inverse, coupling)
    return inverse_panels, inverse_diagonal, inverse_coupling


def swapped(block, axis, bit):
    count = lax.axis_size(axis)
    route = []
    for low in range(count):
        high = low | 1 << bit
        if high != low and high < count:
            route += [(low, high), (high, low)]
    return lax.ppermute(block, axis, route)


def row_masks(pattern_eff, first_row, row_count, block_rows):
    row_index = first_row + jnp.arange(row_count, dtype=jnp.int32)
    blocks = row_index // block_rows
    onehot = (blocks[:, None] == jnp.arange(pattern_eff.shape[1], dtype=jnp.int32)[None, :]).astype(
        jnp.float32
    )
    return matmul(pattern_eff, onehot.T)


def whole_panels(ancestor_inverse, factor_panels, diag_inverse, coupling, block_pattern, tree_order):
    grid_row = lax.axis_index("row")
    grid_col = lax.axis_index("col")
    tile_rows = ancestor_inverse.shape[1]
    half_rows = ancestor_inverse.shape[2]
    piece_rows = factor_panels.shape[2]
    block_rows = factor_panels.shape[3]
    super_count = factor_panels.shape[0]
    share_rows = tile_rows // 2
    sorted_pattern = jnp.take(block_pattern, tree_order, axis=0).astype(jnp.float32)
    pattern_eff = jnp.concatenate(
        [sorted_pattern[:2], sorted_pattern[2:] * sorted_pattern[:2]], axis=0
    )
    source_mask = row_masks(
        pattern_eff, grid_col * half_rows + grid_row * piece_rows, piece_rows, block_rows
    )
    target_mask = row_masks(pattern_eff, grid_row * tile_rows, tile_rows, block_rows)
    panels = jnp.take(factor_panels, tree_order, axis=0) * source_mask[:, None, :, None]
    diag_blocks = jnp.take(diag_inverse, tree_order, axis=0)
    columns = []
    products = []
    for tree_slot in range(super_count):
        gathered = lax.all_gather(panels[tree_slot], "row", axis=1, tiled=True)
        columns.append(gathered)
        products.append(lax.psum(multiply(ancestor_inverse, gathered), "col"))
    own_flag = (grid_row * tile_rows // half_rows == grid_col).astype(jnp.float32)
    offset = jnp.clip(grid_row * tile_rows - grid_col * half_rows, 0, half_rows - tile_rows)
    own_windows = jnp.stack(
        [
            lax.dynamic_slice_in_dim(column_set, offset, tile_rows, 1) * own_flag
            for column_set in columns
        ]
    )
    partner_windows = swapped(own_windows, "col", 0)
    tile_windows = own_windows + partner_windows

    def share(matrix):
        return lax.dynamic_slice_in_dim(matrix, grid_col * share_rows, share_rows, 1)

    windows = [share(tile_windows[tree_slot]) for tree_slot in range(super_count)]
    parent_cols = [
        -target_mask[tree_slot][None, :, None] * products[tree_slot] for tree_slot in range(2)
    ]
    child_cols = [
        -target_mask[tree_slot + 2][None, :, None]
        * (products[tree_slot + 2] + multiply(parent_cols[tree_slot], coupling[tree_slot]))
        for tree_slot in range(2)
    ]
    parent_local = [
        multiply(flipped(windows[tree_slot]), share(parent_cols[tree_slot]))
        for tree_slot in range(2)
    ]
    cross_local = [
        multiply(flipped(share(parent_cols[tree_slot])), windows[tree_slot + 2])
        for tree_slot in range(2)
    ]
    child_local = [
        multiply(flipped(windows[tree_slot + 2]), share(child_cols[tree_slot]))
        for tree_slot in range(2)
    ]
    parent_sums = lax.psum(jnp.stack(parent_local), ("row", "col"))
    parent_diag = [diag_blocks[tree_slot] - parent_sums[tree_slot] for tree_slot in range(2)]
    child_totals = lax.psum(jnp.stack(cross_local + child_local), ("row", "col"))
    crosses = [
        -(child_totals[tree_slot] + multiply(parent_diag[tree_slot], coupling[tree_slot]))
        for tree_slot in range(2)
    ]
    child_sums = [child_totals[2 + tree_slot] for tree_slot in range(2)]
    child_diag = [
        diag_blocks[tree_slot + 2]
        - child_sums[tree_slot]
        - multiply(flipped(coupling[tree_slot]), crosses[tree_slot])
        for tree_slot in range(2)
    ]
    all_cols = jnp.stack(parent_cols + child_cols)
    all_diag = jnp.stack(parent_diag + child_diag)
    inverse_panels = jnp.zeros_like(all_cols).at[tree_order].set(all_cols)
    inverse_diagonal = jnp.zeros_like(all_diag).at[tree_order].set(all_diag)
    return (inverse_panels, inverse_diagonal, jnp.stack(crosses))


def per_device(ancestor_inverse, factor_panels, *others):
    row_count, col_count = lax.axis_size("row"), lax.axis_size("col")
    piece_rows, block = factor_panels.shape[2:]
    tile_rows, half_rows = ancestor_inverse.shape[1:]
    whole_blocks = piece_rows % block == 0 and half_rows % tile_rows == 0
    even_shares = row_count == 2 * LINES and 3 * block % LINES == 0
    if whole_blocks and col_count == 2 and even_shares:
        return live_units(ancestor_inverse, factor_panels, *others)
    return whole_panels(ancestor_inverse, factor_panels, *others)


def solution(mesh):
    return jax.shard_map(
        per_device,
        mesh=mesh,
        in_specs=(
            P(None, ("pole", "row"), "col"),
            P(None, None, ("pole", "col", "row"), None),
            P("pole", None, None, None),
            P("pole", None, None, None),
            P(),
            P(),
        ),
        out_specs=(
            P(None, None, ("pole", "row"), None),
            P("pole", None, None, None),
            P("pole", None, None, None),
        ),
        check_vma=False,
    )
```

```python
import functools

import jax
import jax.numpy as jnp
from jax import lax
from jax.experimental import pallas as pl
from jax.experimental.pallas import tpu as pltpu
from jax.sharding import PartitionSpec as P


def matmul(left_side, right_side):
    return jnp.dot(
        left_side, right_side, preferred_element_type=jnp.float32, precision=lax.Precision.HIGHEST
    )


def multiply(left_side, right_side):
    real_part = matmul(left_side[0], right_side[0]) - matmul(left_side[1], right_side[1])
    imag_part = matmul(left_side[0], right_side[1]) + matmul(left_side[1], right_side[0])
    return jnp.stack([real_part, imag_part])


def flipped(matrix):
    return jnp.swapaxes(matrix, 1, 2)


def halves(value):
    high = value.astype(jnp.bfloat16)
    low = (value - high.astype(jnp.float32)).astype(jnp.bfloat16)
    return high, low


def dot32(left_side, right_side, contract=((1,), (0,))):
    return lax.dot_general(
        left_side, right_side, (contract, ((), ())), preferred_element_type=jnp.float32
    )


def dot3(left_side, right_side, contract=((1,), (0,))):
    return (
        dot32(left_side[0], right_side[0], contract)
        + dot32(left_side[0], right_side[1], contract)
        + dot32(left_side[1], right_side[0], contract)
    )


ARRIVALS = (
    ("own", False, (0, 1, 2, 3)),
    ("right 1", False, (None, 0, 1, 2)),
    ("left 1", False, (1, 2, 3, None)),
    ("over 1", True, (0, 1, 2, 3)),
    ("right 2", False, (None, None, 0, 1)),
    ("left 2", False, (2, 3, None, None)),
    ("out 2", True, (None, 0, 3, None)),
    ("over 2", True, (1, 2, 1, 2)),
    ("right 3", False, (None, None, None, 0)),
    ("left 3", False, (3, None, None, None)),
    ("over 3", True, (2, 3, 0, 1)),
    ("over 4", True, (3, None, None, 0)),
)
LINES = len(ARRIVALS[0][2])


class Layout:
    def __init__(self, rows, cols, a_shape, p_shape):
        self.rows, self.cols = rows, cols
        self.lines = rows // 2
        self.slots, _, self.piece_rows, self.block = p_shape
        self.tile_rows, self.half_rows = a_shape[1:]
        self.piece_blocks = self.piece_rows // self.block
        self.tile_blocks = self.tile_rows // self.block
        self.half_blocks = self.half_rows // self.block
        self.units = self.piece_blocks * self.slots
        self.room = self.units - self.units // 6
        self.spare = self.units - self.room
        self.buffers = len(ARRIVALS)
        self.group = next(size for size in (4, 3, 2, 1) if self.tile_blocks % size == 0)
        self.ranks = 0
        self.source = cols * rows * self.units
        self.order = self.source + self.units
        self.live = self.order + self.slots * self.tile_blocks
        self.owners = self.live + self.slots
        self.windows = self.owners + self.buffers
        self.most = self.windows + 2
        self.total = self.most + 1


def plan_kernel(layout, place, pattern, order, plan):
    row, col = place[0], place[1]
    trees = layout.slots // 2
    names = [order[slot] for slot in range(layout.slots)]

    def live(slot, block):
        value = pattern[names[slot], block]
        if slot >= trees:
            value = value * pattern[names[slot - trees], block]
        return value

    def of_owner(owner, most):
        count = jnp.int32(0)
        for piece in range(layout.piece_blocks):
            for slot in range(layout.slots):
                value = live(slot, owner * layout.piece_blocks + piece)
                at = owner * layout.units + piece * layout.slots + slot
                plan[layout.ranks + at] = jnp.where(value > 0, count, -1)
                count = count + value
        return jnp.maximum(most, count)

    plan[layout.most] = lax.fori_loop(0, layout.cols * layout.rows, of_owner, jnp.int32(0))
    for unit in range(layout.units):
        plan[layout.source + unit] = 0
    mine = (col * layout.rows + row) * layout.units
    for unit in range(layout.units):
        rank = plan[layout.ranks + mine + unit]

        @pl.when(rank >= 0)
        def _():
            plan[layout.source + rank] = unit

    for slot in range(layout.slots):
        count = jnp.int32(0)
        values = []
        for index in range(layout.tile_blocks):
            value = live(slot, row * layout.tile_blocks + index)
            values.append(value)
            count = count + value
        plan[layout.live + slot] = count
        front, back = jnp.int32(0), count
        for index, value in enumerate(values):
            at = layout.order + slot * layout.tile_blocks + jnp.where(value > 0, front, back)
            plan[at] = index
            front, back = front + value, back + 1 - value

    line, side = row // 2, row % 2
    window_line = (row * layout.tile_blocks % layout.half_blocks) // layout.piece_blocks // 2
    windows = [jnp.int32(0), jnp.int32(0)]
    for index, (_, across, origins) in enumerate(ARRIVALS):
        owner = jnp.int32(-1)
        for at, origin in enumerate(origins):
            if origin is not None:
                from_side = 1 - side if across else side
                owner = jnp.where(line == at, origin * 2 + from_side, owner)
        plan[layout.owners + index] = owner
        for which in range(2):
            hit = owner == window_line * 2 + which
            windows[which] = jnp.where(hit, index, windows[which])
    for which in range(2):
        plan[layout.windows + which] = windows[which]


def make_plan(layout, row, col, block_pattern, tree_order):
    smem = pl.BlockSpec(memory_space=pltpu.SMEM)
    return pl.pallas_call(
        functools.partial(plan_kernel, layout),
        out_shape=jax.ShapeDtypeStruct((layout.total,), jnp.int32),
        in_specs=[smem] * 3,
        out_specs=smem,
        name="make_plan",
    )(jnp.stack([row, col]).astype(jnp.int32), block_pattern, tree_order)


def compact_kernel(layout, plan, order, panels, units, spare, sems):
    block = layout.block
    copies = []
    for unit in range(layout.units):
        source = plan[layout.source + unit]
        first = pl.multiple_of(source // layout.slots * block, block)
        inside = unit < layout.room
        copy = pltpu.make_async_copy(
            panels.at[order[source % layout.slots], :, pl.ds(first, block), :],
            units.at[unit] if inside else spare.at[unit - layout.room],
            sems.at[unit],
        )
        copy.start()
        copies.append(copy)
    for copy in copies:
        copy.wait()


def compact_units(layout, plan, tree_order, panels):
    shapes = [(count, 2, layout.block, layout.block) for count in (layout.room, layout.spare)]
    return pl.pallas_call(
        functools.partial(compact_kernel, layout),
        out_shape=[jax.ShapeDtypeStruct(shape, jnp.float32) for shape in shapes],
        grid_spec=pltpu.PrefetchScalarGridSpec(
            num_scalar_prefetch=2,
            grid=(1,),
            in_specs=[pl.BlockSpec(memory_space=pltpu.HBM)],
            out_specs=[pl.BlockSpec(shape, lambda step, *_: (0, 0, 0, 0)) for shape in shapes],
            scratch_shapes=[pltpu.SemaphoreType.DMA((layout.units,))],
        ),
        compiler_params=pltpu.CompilerParams(vmem_limit_bytes=16 * 2**20),
        name="compact_units",
    )(plan, tree_order, panels)


def owner_at(layout, which, plan, step):
    if which is None:
        return step // layout.piece_blocks
    owner = plan[layout.owners + which[0]]
    for local in range(1, len(which)):
        later = step // layout.piece_blocks >= local
        owner = jnp.where(later, plan[layout.owners + which[local]], owner)
    return owner


def gemm_kernel(layout, which, parted, first_call, plan, place, *refs):
    refs = list(refs)
    in_ref = None if first_call else refs.pop(0)
    a_ref = refs.pop(0)
    *units, out_ref, total, a_parts, weights, sems = refs
    step = pl.program_id(0)
    block, rows = layout.block, layout.tile_rows
    width = 2 * block
    span_rows = layout.group * block

    def each_slot(source, target, act):
        for slot in range(layout.slots):
            getattr(pltpu.make_async_copy(source.at[slot], target.at[slot], sems.at[slot]), act)()

    @pl.when(step == 0)
    def _():
        if first_call:
            total[: layout.slots] = jnp.zeros((layout.slots, rows, width), jnp.float32)
        else:
            each_slot(in_ref, total, "start")

    owner = owner_at(layout, which, plan, step)

    @pl.loop(0, jnp.where(owner >= 0, rows // block, 0))
    def _(index):
        span = pl.ds(pl.multiple_of(index * block, block), block)
        for part in range(2):
            high, low = halves(a_ref[part, span, :])
            a_parts[span, part * block : (part + 1) * block] = high
            a_parts[span, width + part * block : width + (part + 1) * block] = low
            a_parts[span, 2 * width + part * block : 2 * width + (part + 1) * block] = high

    if not first_call:

        @pl.when(step == 0)
        def _():
            each_slot(in_ref, total, "wait")

    base = place[1] * layout.rows * layout.units + jnp.maximum(owner, 0) * layout.units
    base = base + step % layout.piece_blocks * layout.slots
    front = units[0].shape[0]

    def places(rank):
        if which is None:
            return [(rank >= layout.room, lambda: units[0].at[owner, rank - layout.room])]
        if parted:
            lower = place[0] // 2 < LINES // 2
            inside, outside = (rank >= 0) & (rank < front), (rank >= front) & (rank < layout.room)
            return [
                (inside, lambda: units[0].at[rank]),
                (outside & ~lower, lambda: units[1].at[rank - front]),
                (outside & lower, lambda: units[2].at[rank - front]),
            ]
        inside = (rank >= 0) & (rank < layout.room)
        found = []
        for local, ref in enumerate(units):
            here = inside & (step // layout.piece_blocks == local)
            found.append((here, lambda ref=ref: ref.at[rank]))
        return found

    count = jnp.int32(0)
    chosen = [jnp.int32(layout.slots)] * layout.slots
    for slot in range(layout.slots):
        rank = plan[layout.ranks + base + slot]
        wanted = rank >= layout.room if which is None else (rank >= 0) & (rank < layout.room)
        wanted = wanted & (owner >= 0) & (plan[layout.live + slot] > 0)
        for at in range(layout.slots):
            chosen[at] = jnp.where(wanted & (count == at), slot, chosen[at])
        count = count + wanted.astype(jnp.int32)

    @pl.loop(0, (count + 1) // 2)
    def _(pair):
        slots = []
        for side in range(2):
            slot = chosen[side]
            for at in range(2 + side, layout.slots, 2):
                slot = jnp.where(pair == at // 2, chosen[at], slot)
            slots.append(slot)
            used = slot < layout.slots
            rank = plan[layout.ranks + base + jnp.minimum(slot, layout.slots - 1)]
            left = slice(side * width, side * width + block)
            middle = slice(side * width + block, (side + 1) * width)

            for here, find in places(rank):

                @pl.when(used & here)
                def _():
                    unit = find()
                    real, imag = unit[0], unit[1]
                    real_parts, imag_parts = halves(real), halves(imag)
                    for third, part in enumerate((0, 0, 1)):
                        upper = slice(third * width, third * width + block)
                        lower = slice(third * width + block, (third + 1) * width)
                        weights[upper, left] = real_parts[part]
                        weights[upper, middle] = imag_parts[part]
                        weights[lower, left] = -imag_parts[part]
                        weights[lower, middle] = real_parts[part]

        @pl.loop(0, rows // span_rows)
        def _(index):
            span = pl.ds(pl.multiple_of(index * span_rows, span_rows), span_rows)
            product = dot32(a_parts[span, :], weights[...])
            for side in range(2):
                total[slots[side], span, :] += product[:, side * width : (side + 1) * width]

    @pl.when(step == pl.num_programs(0) - 1)
    def _():
        each_slot(total, out_ref, "start")
        each_slot(total, out_ref, "wait")


def gemm_units(layout, plan, place, total, ancestor_inverse, buffers, which, parted=False):
    first_call = total is None
    totals = [] if first_call else [total]
    hbm = pl.BlockSpec(memory_space=pltpu.HBM)
    block, pieces = layout.block, layout.piece_blocks
    rows, width = layout.tile_rows, 2 * layout.block

    def column(step, plan, place):
        owner = owner_at(layout, which, plan, step)
        return 0, 0, jnp.where(owner >= 0, owner * pieces + step % pieces, 0)

    shape = (layout.slots, rows, width)
    steps = (layout.rows if which is None else len(which)) * pieces
    return pl.pallas_call(
        functools.partial(gemm_kernel, layout, which, parted, first_call),
        out_shape=jax.ShapeDtypeStruct(shape, jnp.float32),
        grid_spec=pltpu.PrefetchScalarGridSpec(
            num_scalar_prefetch=2,
            grid=(steps,),
            in_specs=[hbm] * len(totals)
            + [pl.BlockSpec((2, rows, block), column)]
            + [
                pl.BlockSpec(
                    buffer.shape,
                    lambda step, plan, place, rank=buffer.ndim: (0,) * rank,
                    pipeline_mode=pl.Buffered(1),
                )
                for buffer in buffers
            ],
            out_specs=hbm,
            scratch_shapes=[
                pltpu.VMEM((layout.slots + 1, rows, width), jnp.float32),
                pltpu.VMEM((rows, 3 * width), jnp.bfloat16),
                pltpu.VMEM((3 * width, 2 * width), jnp.bfloat16),
                pltpu.SemaphoreType.DMA((layout.slots,)),
            ],
        ),
        input_output_aliases={} if first_call else {2: 0},
        compiler_params=pltpu.CompilerParams(vmem_limit_bytes=36 * 2**20),
        cost_estimate=pl.CostEstimate(
            flops=steps * layout.slots * 3 * 2 * rows * width * width // 2,
            bytes_accessed=steps * rows * block * 8 + 8 * layout.slots * rows * width,
            transcendentals=0,
        ),
        name="gemm_units",
    )(plan, place, *totals, ancestor_inverse, *buffers)


def window_kernel(layout, plan, place, *refs):
    buffers, (spare, out, sems) = refs[: layout.buffers - 1], refs[layout.buffers - 1 :]
    row, col = place[0], place[1]
    holds = row * layout.tile_blocks // layout.half_blocks == col
    owner = row * layout.tile_blocks % layout.half_blocks // layout.piece_blocks
    beyond = plan[layout.most] > layout.room

    def fetch(which, index):
        target = out.at[which, pl.ds(0, layout.room)]
        return pltpu.make_async_copy(buffers[index], target, sems.at[which])

    def fetch_spare(which):
        target = out.at[which, pl.ds(layout.room, layout.spare)]
        return pltpu.make_async_copy(spare.at[owner + which], target, sems.at[2 + which])

    for act in ("start", "wait"):
        for which in range(2):
            for index in range(layout.buffers - 1):

                @pl.when(holds & (plan[layout.windows + which] == index))
                def _():
                    getattr(fetch(which, index), act)()

            @pl.when(holds & beyond)
            def _():
                getattr(fetch_spare(which), act)()


def find_windows(layout, plan, place, buffers, spare):
    shape = (2, layout.units, 2, layout.block, layout.block)
    return pl.pallas_call(
        functools.partial(window_kernel, layout),
        out_shape=jax.ShapeDtypeStruct(shape, jnp.float32),
        grid_spec=pltpu.PrefetchScalarGridSpec(
            num_scalar_prefetch=2,
            grid=(1,),
            in_specs=[pl.BlockSpec(memory_space=pl.ANY)] * layout.buffers,
            out_specs=pl.BlockSpec(shape, lambda step, *_: (0, 0, 0, 0, 0)),
            scratch_shapes=[pltpu.SemaphoreType.DMA((4,))],
        ),
        compiler_params=pltpu.CompilerParams(vmem_limit_bytes=16 * 2**20),
        name="find_windows",
    )(plan, place, *buffers, spare)


def contract_kernel(layout, step_blocks, plan, place, mine, near, far, sums, acc, held, sem):
    step = pl.program_id(0)
    block, slots, trees = layout.block, layout.slots, layout.slots // 2
    row, col = place[0], place[1]
    half = row * layout.tile_blocks // layout.half_blocks
    inner = row * layout.tile_blocks % layout.half_blocks
    base = half * layout.rows * layout.units + inner * slots

    @pl.when(step == 0)
    def _():
        acc[...] = jnp.zeros_like(acc)
        for source, here in ((near, half == col), (far, half != col)):

            @pl.when(here)
            def _():
                copy = pltpu.make_async_copy(source, held, sem)
                copy.start()
                copy.wait()

    def window(slot):
        parts = []
        for at in range(step_blocks):
            index = step * step_blocks + at
            rank = plan[layout.ranks + base + index * slots + slot]
            unit = held.at[index // layout.piece_blocks, jnp.maximum(rank, 0)]
            whole = jnp.concatenate([unit[0], unit[1]], axis=1)
            parts.append(jnp.where(rank >= 0, -whole, 0.0))
        return halves(jnp.concatenate(parts, axis=0))

    rows_first = ((0,), (0,))

    @pl.loop(0, trees)
    def _(tree):
        child = tree + trees
        parent_parts = halves(mine[tree])
        child_panel = window(child)
        acc[3 * tree] += dot3(window(tree), parent_parts, rows_first)
        acc[3 * tree + 1] += dot3(child_panel, parent_parts, rows_first)
        acc[3 * tree + 2] += dot3(child_panel, halves(mine[child]), rows_first)

    @pl.when(step == pl.num_programs(0) - 1)
    def _():
        for index in range(3 * trees):
            value = acc[index]
            sums[index, 0] = value[:block, :block] - value[block:, block:]
            sums[index, 1] = value[:block, block:] + value[block:, :block]


def contract_windows(layout, plan, place, mine, near, far):
    block, slots = layout.block, layout.slots
    rows, width = layout.tile_rows, 2 * layout.block
    step_blocks = layout.group
    step_rows = step_blocks * block
    sums_shape = (3 * slots // 2, 2, block, block)
    return pl.pallas_call(
        functools.partial(contract_kernel, layout, step_blocks),
        out_shape=jax.ShapeDtypeStruct(sums_shape, jnp.float32),
        grid_spec=pltpu.PrefetchScalarGridSpec(
            num_scalar_prefetch=2,
            grid=(rows // step_rows,),
            in_specs=[pl.BlockSpec((slots, step_rows, width), lambda step, *_: (0, step, 0))]
            + [pl.BlockSpec(memory_space=pl.ANY)] * 2,
            out_specs=pl.BlockSpec(sums_shape, lambda step, *_: (0, 0, 0, 0)),
            scratch_shapes=[
                pltpu.VMEM((3 * slots // 2, width, width), jnp.float32),
                pltpu.VMEM(near.shape, jnp.float32),
                pltpu.SemaphoreType.DMA,
            ],
        ),
        compiler_params=pltpu.CompilerParams(vmem_limit_bytes=24 * 2**20),
        name="contract_windows",
    )(plan, place, mine, near, far)


def column_kernel(layout, step_blocks, first_step, plan, order, mine, other, coupling, *refs):
    step = pl.program_id(0) + first_step
    block, trees = layout.block, layout.slots // 2
    columns = refs[-1]

    def masked(slot, value):
        parts = []
        for at in range(step_blocks):
            alive = is_live(slot, step * step_blocks + at)
            parts.append(jnp.where(alive, -value[at * block : (at + 1) * block], 0.0))
        return jnp.concatenate(parts, axis=0)

    def is_live(slot, index):
        alive = jnp.bool_(False)
        for at in range(layout.tile_blocks):
            found = plan[layout.order + slot * layout.tile_blocks + at] == index
            alive = alive | (found & (at < plan[layout.live + slot]))
        return alive

    def put(slot, value):
        columns[order[slot], 0] = value[:, :block]
        columns[order[slot], 1] = value[:, block:]

    @pl.loop(0, trees)
    def _(tree):
        child = tree + trees
        real, imag = coupling[tree, 0], coupling[tree, 1]
        link = jnp.concatenate(
            [jnp.concatenate([real, imag], axis=1), jnp.concatenate([-imag, real], axis=1)], axis=0
        )
        parent_col = masked(tree, mine[tree] + other[tree])
        put(tree, parent_col)
        linked = dot3(halves(parent_col), halves(link))
        put(child, masked(child, mine[child] + other[child] + linked))


def finish_columns(layout, plan, tree_order, mine, other, coupling, begun=None):
    block, slots = layout.block, layout.slots
    rows, width = layout.tile_rows, 2 * layout.block
    step_blocks = 2 if layout.tile_blocks % 2 == 0 else 1
    step_rows = step_blocks * block
    steps = rows // step_rows
    first_step = 0 if begun is None else steps // 2
    count = steps // 2 if begun is None else steps - steps // 2
    half = pl.BlockSpec((slots, step_rows, width), lambda step, *_: (0, step + first_step, 0))
    return pl.pallas_call(
        functools.partial(column_kernel, layout, step_blocks, first_step),
        out_shape=jax.ShapeDtypeStruct((slots, 2, rows, block), jnp.float32),
        grid_spec=pltpu.PrefetchScalarGridSpec(
            num_scalar_prefetch=2,
            grid=(count,),
            in_specs=[half, half, pl.BlockSpec(coupling.shape, lambda step, *_: (0, 0, 0, 0))]
            + ([] if begun is None else [pl.BlockSpec(memory_space=pl.ANY)]),
            out_specs=pl.BlockSpec(
                (slots, 2, step_rows, block), lambda step, *_: (0, 0, step + first_step, 0)
            ),
        ),
        input_output_aliases={} if begun is None else {5: 0},
        compiler_params=pltpu.CompilerParams(vmem_limit_bytes=16 * 2**20),
        cost_estimate=pl.CostEstimate(
            flops=slots * 3 * rows * width * width // 2,
            bytes_accessed=6 * slots * rows * width,
            transcendentals=0,
        ),
        name="finish_columns",
    )(plan, tree_order, mine, other, coupling, *([] if begun is None else [begun]))


def complex_dot(left_side, right_side, contract=((1,), (0,))):
    def dot(left_part, right_part):
        return dot3(halves(left_side[left_part]), halves(right_side[right_part]), contract)

    return dot(0, 0) - dot(1, 1), dot(0, 1) + dot(1, 0)


def diagonal_kernel(order, sums, diag_in, coupling, diag_out, cross_out):
    trees = coupling.shape[0]
    for tree in range(trees):
        parent, child = order[tree], order[tree + trees]
        link = (coupling[tree, 0], coupling[tree, 1])
        parent_diag = tuple(diag_in[parent, part] - sums[3 * tree, part] for part in range(2))
        moved = complex_dot(parent_diag, link)
        between = tuple(sums[3 * tree + 1, part] for part in range(2))
        linked = complex_dot(between, link)
        cross = tuple(-(between[part].T + moved[part]) for part in range(2))
        back = complex_dot(link, cross, ((0,), (0,)))
        for part in range(2):
            diag_out[parent, part] = parent_diag[part]
            cross_out[tree, part] = cross[part]
            child_sum = sums[3 * tree + 2, part] - linked[part]
            diag_out[child, part] = diag_in[child, part] - child_sum - back[part]


def finish_diagonals(order, sums, diag_inverse, coupling):
    vmem = pl.BlockSpec(memory_space=pltpu.VMEM)
    return pl.pallas_call(
        diagonal_kernel,
        out_shape=(
            jax.ShapeDtypeStruct(diag_inverse.shape, jnp.float32),
            jax.ShapeDtypeStruct(coupling.shape, jnp.float32),
        ),
        in_specs=[pl.BlockSpec(memory_space=pltpu.SMEM), vmem, vmem, vmem],
        out_specs=(vmem, vmem),
        name="finish_diagonals",
    )(order, sums, diag_inverse, coupling)


def along(value, lines, step):
    route = [(2 * at + side, 2 * (at + step) + side) for at in lines for side in range(2)]
    return lax.ppermute(value, "row", route)


def swap(value, axis):
    return lax.ppermute(value, axis, [(at, at ^ 1) for at in range(lax.axis_size(axis))])


def pick(values, index):
    return lax.dynamic_index_in_dim(values, index, 0, keepdims=False)


def sum_devices(layout, sums, row, col, begin, end):
    lines, line, side = layout.lines, row // 2, row % 2
    parts = sums.reshape(2, 2, lines, -1, layout.block)
    mine = pick(parts, col) + swap(pick(parts, 1 - col), "col")
    came, beside = lax.optimization_barrier((swap(pick(mine, 1 - side), "row"), begin()))
    mine = pick(mine, side) + came

    def turn(value, by):
        route = [
            (2 * at + side, 2 * ((at + by) % lines) + side)
            for at in range(lines)
            for side in range(2)
        ]
        return lax.ppermute(value, "row", route)

    came = [turn(pick(mine, (line + by) % lines), by) for by in range(1, lines)]
    came, beside = lax.optimization_barrier((came, end(beside)))
    share = sum(came, pick(mine, line))
    others = [share] + [turn(share, by) for by in range(1, lines)]
    stacked = jnp.stack(others)
    whole = jnp.zeros_like(stacked)
    for by in range(lines):
        whole = lax.dynamic_update_index_in_dim(whole, others[by], (line - by) % lines, 0)
    far = swap(whole, "row")
    sides = jnp.stack([jnp.where(side == 0, whole, far), jnp.where(side == 0, far, whole)])
    opposite = swap(sides, "col")
    trees = jnp.stack([jnp.where(col == 0, sides, opposite), jnp.where(col == 0, opposite, sides)])
    return trees.reshape(sums.shape), beside


def live_units(ancestor_inverse, factor_panels, diag_inverse, coupling, block_pattern, tree_order):
    layout = Layout(
        lax.axis_size("row"), lax.axis_size("col"), ancestor_inverse.shape, factor_panels.shape
    )
    row, col = lax.axis_index("row"), lax.axis_index("col")
    place = jnp.stack([row, col]).astype(jnp.int32)
    line = row // 2
    plan = make_plan(layout, row, col, block_pattern, tree_order)
    room = layout.room
    own, spare = compact_units(layout, plan, tree_order, factor_panels)
    half = room // 2

    def multiplied(total, buffers, first):
        which = None if first is None else list(range(first, first + len(buffers)))
        return gemm_units(layout, plan, place, total, ancestor_inverse, buffers, which)

    def phase(came, total, buffers, first):
        return lax.optimization_barrier((came, multiplied(total, buffers, first)))

    def inward(values):
        return jnp.where(line < LINES // 2, values[1], values[0])

    came = along(own, range(LINES - 1), 1), along(own, range(1, LINES), -1), swap(own, "row")
    first, total = phase(came, None, [own], 0)

    def beyond(_, state):
        gathered = lax.all_gather(spare, "row", axis=0, tiled=False)
        return gathered, multiplied(state[1], [gathered], None)

    trips = (plan[layout.most] > room).astype(jnp.int32)
    spares = jnp.zeros((layout.rows,) + spare.shape, jnp.float32)
    spares, total = lax.fori_loop(0, trips, beyond, (spares, total))

    end = LINES - 1
    came = along(first[0], range(1, end), 1), along(first[1], range(1, end), -1)
    outward = [(at, at + 2) for at in range(2)] + [(at + 2 * end, at + 2 * end - 2) for at in range(2)]
    came += lax.ppermute(first[2], "row", outward), swap(inward(first), "row")
    second, total = phase(came, total, list(first), 1)
    came = along(second[0], [end - 1], 1), along(second[1], [1], -1), swap(inward(second), "row")
    third, total = phase(came, total, list(second), 4)
    rest = lax.slice_in_dim(third[2], room - half, room, axis=0)
    over = lax.slice_in_dim(inward(third), 0, room - half, axis=0)
    came = along(rest, [end - 1], 1), along(rest, [1], -1), swap(over, "row")
    total = multiplied(total, list(third), 8)
    third, total = lax.optimization_barrier((third, total))
    near = find_windows(layout, plan, place, [own, *first, *second, *third], spares)
    far = swap(near, "col")
    last, total, near = lax.optimization_barrier((came, total, near))
    last = [last[2], last[0], last[1]]
    total = gemm_units(layout, plan, place, total, ancestor_inverse, last, [11], parted=True)

    other = swap(total, "col")
    sums = contract_windows(layout, plan, place, total, near, far)
    other, sums = lax.optimization_barrier((other, sums))
    columns = functools.partial(finish_columns, layout, plan, tree_order, total, other, coupling)
    sums, inverse_panels = sum_devices(layout, sums, row, col, columns, columns)
    inverse_diagonal, inverse_coupling = finish_diagonals(tree_order, sums, diag_inverse, coupling)
    return inverse_panels, inverse_diagonal, inverse_coupling


def swapped(block, axis, bit):
    count = lax.axis_size(axis)
    route = []
    for low in range(count):
        high = low | 1 << bit
        if high != low and high < count:
            route += [(low, high), (high, low)]
    return lax.ppermute(block, axis, route)


def row_masks(pattern_eff, first_row, row_count, block_rows):
    row_index = first_row + jnp.arange(row_count, dtype=jnp.int32)
    blocks = row_index // block_rows
    onehot = (blocks[:, None] == jnp.arange(pattern_eff.shape[1], dtype=jnp.int32)[None, :]).astype(
        jnp.float32
    )
    return matmul(pattern_eff, onehot.T)


def whole_panels(ancestor_inverse, factor_panels, diag_inverse, coupling, block_pattern, tree_order):
    grid_row = lax.axis_index("row")
    grid_col = lax.axis_index("col")
    tile_rows = ancestor_inverse.shape[1]
    half_rows = ancestor_inverse.shape[2]
    piece_rows = factor_panels.shape[2]
    block_rows = factor_panels.shape[3]
    super_count = factor_panels.shape[0]
    share_rows = tile_rows // 2
    sorted_pattern = jnp.take(block_pattern, tree_order, axis=0).astype(jnp.float32)
    pattern_eff = jnp.concatenate(
        [sorted_pattern[:2], sorted_pattern[2:] * sorted_pattern[:2]], axis=0
    )
    source_mask = row_masks(
        pattern_eff, grid_col * half_rows + grid_row * piece_rows, piece_rows, block_rows
    )
    target_mask = row_masks(pattern_eff, grid_row * tile_rows, tile_rows, block_rows)
    panels = jnp.take(factor_panels, tree_order, axis=0) * source_mask[:, None, :, None]
    diag_blocks = jnp.take(diag_inverse, tree_order, axis=0)
    columns = []
    products = []
    for tree_slot in range(super_count):
        gathered = lax.all_gather(panels[tree_slot], "row", axis=1, tiled=True)
        columns.append(gathered)
        products.append(lax.psum(multiply(ancestor_inverse, gathered), "col"))
    own_flag = (grid_row * tile_rows // half_rows == grid_col).astype(jnp.float32)
    offset = jnp.clip(grid_row * tile_rows - grid_col * half_rows, 0, half_rows - tile_rows)
    own_windows = jnp.stack(
        [
            lax.dynamic_slice_in_dim(column_set, offset, tile_rows, 1) * own_flag
            for column_set in columns
        ]
    )
    partner_windows = swapped(own_windows, "col", 0)
    tile_windows = own_windows + partner_windows

    def share(matrix):
        return lax.dynamic_slice_in_dim(matrix, grid_col * share_rows, share_rows, 1)

    windows = [share(tile_windows[tree_slot]) for tree_slot in range(super_count)]
    parent_cols = [
        -target_mask[tree_slot][None, :, None] * products[tree_slot] for tree_slot in range(2)
    ]
    child_cols = [
        -target_mask[tree_slot + 2][None, :, None]
        * (products[tree_slot + 2] + multiply(parent_cols[tree_slot], coupling[tree_slot]))
        for tree_slot in range(2)
    ]
    parent_local = [
        multiply(flipped(windows[tree_slot]), share(parent_cols[tree_slot]))
        for tree_slot in range(2)
    ]
    cross_local = [
        multiply(flipped(share(parent_cols[tree_slot])), windows[tree_slot + 2])
        for tree_slot in range(2)
    ]
    child_local = [
        multiply(flipped(windows[tree_slot + 2]), share(child_cols[tree_slot]))
        for tree_slot in range(2)
    ]
    parent_sums = lax.psum(jnp.stack(parent_local), ("row", "col"))
    parent_diag = [diag_blocks[tree_slot] - parent_sums[tree_slot] for tree_slot in range(2)]
    child_totals = lax.psum(jnp.stack(cross_local + child_local), ("row", "col"))
    crosses = [
        -(child_totals[tree_slot] + multiply(parent_diag[tree_slot], coupling[tree_slot]))
        for tree_slot in range(2)
    ]
    child_sums = [child_totals[2 + tree_slot] for tree_slot in range(2)]
    child_diag = [
        diag_blocks[tree_slot + 2]
        - child_sums[tree_slot]
        - multiply(flipped(coupling[tree_slot]), crosses[tree_slot])
        for tree_slot in range(2)
    ]
    all_cols = jnp.stack(parent_cols + child_cols)
    all_diag = jnp.stack(parent_diag + child_diag)
    inverse_panels = jnp.zeros_like(all_cols).at[tree_order].set(all_cols)
    inverse_diagonal = jnp.zeros_like(all_diag).at[tree_order].set(all_diag)
    return (inverse_panels, inverse_diagonal, jnp.stack(crosses))


def per_device(ancestor_inverse, factor_panels, *others):
    row_count, col_count = lax.axis_size("row"), lax.axis_size("col")
    piece_rows, block = factor_panels.shape[2:]
    tile_rows, half_rows = ancestor_inverse.shape[1:]
    whole_blocks = piece_rows % block == 0 and half_rows % tile_rows == 0
    even_shares = row_count == 2 * LINES and 3 * block % LINES == 0
    if whole_blocks and col_count == 2 and even_shares:
        return live_units(ancestor_inverse, factor_panels, *others)
    return whole_panels(ancestor_inverse, factor_panels, *others)


def solution(mesh):
    return jax.shard_map(
        per_device,
        mesh=mesh,
        in_specs=(
            P(None, ("pole", "row"), "col"),
            P(None, None, ("pole", "col", "row"), None),
            P("pole", None, None, None),
            P("pole", None, None, None),
            P(),
            P(),
        ),
        out_specs=(
            P(None, None, ("pole", "row"), None),
            P("pole", None, None, None),
            P("pole", None, None, None),
        ),
        check_vma=False,
    )
```
